32 devices in a mesh: feat: 16 (over z, y, x), rep: 2 (over core).
Axes of the slice: x: 2, y: 2, z: 4, core: 2. Of those that a mesh axis runs over, the one named last changes fastest.
Arguments:
- features: bfloat16 [2048, 10, 2048], P('feat', 'rep'), may hold values from -6 to 6
- adjacency: bfloat16 [10, 2048, 2048], P('rep'), may hold values from 0 to 1, as said below
- counts: int32 [10], P('rep'), may hold values from 600 to 2048, as said below
- weight: bfloat16 [2048, 2048], replicated, may hold values from -0.125 to 0.125
- bias: bfloat16 [2048], replicated, may hold values from -3 to 3
- cotangent: bfloat16 [2048, 10, 2048], P('feat', 'rep'), may hold values from -6 to 6
Outputs:
- activations: float32 [2048, 10, 2048], P('feat', 'rep')
- grad_features: float32 [2048, 10, 2048], P('feat', 'rep')
- grad_weight: float32 [2048, 2048], replicated
- grad_bias: float32 [2048], replicated
The draws below stay inside these ranges and needn't reach their ends.
Inputs may be any that keep to these rules, and one draw needn't show every extreme that they name: `counts`: every index of rep holds 5 clusters, one of which has all 2048 nodes live. `adjacency`: Nonnegative; rows and columns of slots at or beyond a cluster's count are zero.
All inputs are finite; a program needn't handle non-finite values.
Results may differ from the reference program's by a relative error of at most 0.005.
Values may be sent and summed in bfloat16 or wider, within the bound.
No kernel may reach another device: no remote copies, remote signals or barrier semaphores. Data moves between devices by JAX's collectives and lax.ppermute only.
A program may use at most 256 MiB of HBM per device.

```python
import jax
import jax.numpy as jnp
from jax import lax

F = 2048
NODES = 2048
MIN_NODES = 600
CL_DEV = 5
CLUSTERS = 10


def cluster_counts(key):
    groups = CLUSTERS // CL_DEV
    key_sizes, key_full = jax.random.split(jax.random.fold_in(key, 17))
    sizes = jax.random.randint(key_sizes, (groups, CL_DEV), MIN_NODES, NODES + 1)
    full_slot = jax.random.randint(key_full, (groups, 1), 0, CL_DEV)
    slot = lax.broadcasted_iota(jnp.int32, (groups, CL_DEV), 1)
    group = lax.broadcasted_iota(jnp.int32, (groups, CL_DEV), 0)
    sizes = jnp.where(slot == full_slot, NODES, sizes)
    if CL_DEV > 1:
        least_slot = (full_slot[0, 0] + 1) % CL_DEV
        sizes = jnp.where((group == 0) & (slot == least_slot), MIN_NODES, sizes)
    return sizes.reshape(CLUSTERS).astype(jnp.int32)


def draw_counts(key, part):
    return cluster_counts(key)


def draw_adjacency(key, part):
    sizes = cluster_counts(key)
    key = jax.random.fold_in(key, 5)
    key_diag, key_near, key_value = jax.random.split(key, 3)
    shape = (CLUSTERS, NODES, NODES)
    row_ids = lax.broadcasted_iota(jnp.int32, shape, 1)
    col_ids = lax.broadcasted_iota(jnp.int32, shape, 2)
    limit = sizes[:, None, None]
    live = (row_ids < limit) & (col_ids < limit)
    diag_vals = 0.5 + 0.5 * jax.random.uniform(key_diag, shape, jnp.float32)
    chance = 4.0 / sizes.astype(jnp.float32)[:, None, None]
    near = jax.random.uniform(key_near, shape, jnp.float32) < chance
    off_vals = 0.1 + 0.2 * jax.random.uniform(key_value, shape, jnp.float32)
    values = jnp.where(row_ids == col_ids, diag_vals, jnp.where(near, off_vals, 0.0))
    return jnp.where(live, values, 0.0).astype(jnp.bfloat16)


def block_levels(own_key, extent, pieces, smallest, high):
    def one(position, shards_of):
        draws = jax.random.uniform(jax.random.fold_in(jax.random.fold_in(own_key, 6), position), (shards_of,), jnp.float32, smallest / len(pieces), high / len(pieces))
        return jnp.repeat(jnp.exp(draws), extent[position] // shards_of).reshape((-1,) + (1,) * (len(extent) - position - 1))

    factor_of = one(*pieces[0])
    for cut in pieces[1:]:
        factor_of = factor_of * one(*cut)
    return factor_of


def scatter_about(rng, shape, deviation, bound, shards=(), held_as=jnp.bfloat16):
    values = deviation * jax.random.normal(rng, shape, jnp.float32)
    if shards:
        values = values * block_levels(rng, shape, shards, -0.22, 0.18)
    return jnp.clip(values, -bound, bound).astype(held_as)


def setup_inputs(seed: int = 0) -> dict:
    key_of = jax.random.split(jax.random.key(seed), 7)
    features = scatter_about(key_of[0], (F, CLUSTERS, NODES), 1.0, 6.0, ((0, 16), (1, 2)))
    adjacency = draw_adjacency(jax.random.fold_in(key_of[6], 71), 0)
    counts = draw_counts(jax.random.fold_in(key_of[6], 71), 0)
    weight = scatter_about(key_of[3], (F, F), F ** -0.5, 0.125)
    bias = scatter_about(key_of[4], (F,), 0.5, 3.0)
    cotangent = scatter_about(key_of[5], (F, CLUSTERS, NODES), 1.0, 6.0, ((0, 16), (1, 2)))
    return dict(features=features, adjacency=adjacency, counts=counts, weight=weight, bias=bias, cotangent=cotangent)


@jax.custom_vjp
def low(v):
    return lax.optimization_barrier(v.astype(jnp.bfloat16)).astype(jnp.float32)

@jax.custom_vjp
def low_back(v):
    return v

def low_keep(v):
    return (low(v), None)

def low_pass(kept, grad):
    return (grad,)

def back_keep(v):
    return (v, None)

def back_low(kept, grad):
    return (low(grad),)
low.defvjp(low_keep, low_pass)
low_back.defvjp(back_keep, back_low)

def forward(inputs, weight, bias, adjacency, mask):
    masked = inputs * mask[None]
    diagonal = jnp.diagonal(adjacency, axis1=1, axis2=2)
    aggregated = jnp.einsum('fcj,cij->fci', masked, adjacency, precision=lax.Precision.HIGHEST)
    aggregated = aggregated + diagonal[None] * masked
    aggregated = low_back(low(aggregated))
    product = jnp.einsum('fg,fcn->gcn', weight, aggregated, precision=lax.Precision.HIGHEST)
    pre = low_back(product) + bias[:, None, None]
    return mask[None] * jax.nn.gelu(pre, approximate=False)

def reference(features, adjacency, counts, weight, bias, cotangent):
    slots = lax.broadcasted_iota(jnp.int32, (counts.shape[0], features.shape[2]), 1)
    mask = (slots < counts[:, None]).astype(jnp.float32)
    adj_full = adjacency.astype(jnp.float32)

    def apply(inputs, matrix, shift):
        return forward(inputs, matrix, shift, adj_full, mask)
    activations, pullback = jax.vjp(apply, features.astype(jnp.float32), weight.astype(jnp.float32), bias.astype(jnp.float32))
    grad_features, grad_weight, grad_bias = pullback(cotangent.astype(jnp.float32))
    return (activations, grad_features, grad_weight, grad_bias)
```

```python
import functools

import jax
import jax.numpy as jnp
from jax import lax
from jax.experimental import pallas as pl
from jax.experimental.pallas import tpu as pltpu
from jax.sharding import PartitionSpec as P

TILE = 128
ROWS = 512
F32 = jnp.float32
BF16 = jnp.bfloat16
BUCKETS = (40, 48, 56, 64, 72, 80)


def params(mib=48):
    return pltpu.CompilerParams(vmem_limit_bytes=mib * 1024 * 1024)


def cost(flops, moved, transcendentals=0):
    return pl.CostEstimate(flops=flops, bytes_accessed=moved, transcendentals=transcendentals)


def dot(a, b, ca, cb):
    return lax.dot_general(a, b, (((ca,), (cb,)), ((), ())), preferred_element_type=F32)


def eye():
    row = lax.broadcasted_iota(jnp.int32, (TILE, TILE), 0)
    return row == lax.broadcasted_iota(jnp.int32, (TILE, TILE), 1)


def aligned(index, size=TILE):
    return pl.ds(pl.multiple_of(index * TILE, TILE), size)


def clear_tail(out_ref, first, last):
    def body(p, carry):
        out_ref[aligned(p), :] = jnp.zeros((TILE, out_ref.shape[1]), out_ref.dtype)
        return carry

    lax.fori_loop(first, last, body, 0)


def pack_kernel(clusters, counts, offsets, in_ref, out_ref):
    features = in_ref.shape[1]
    for c in range(clusters):
        live = counts[c]
        start = offsets[c]

        def body(t, carry):
            lane = t * TILE + lax.broadcasted_iota(jnp.int32, (features, TILE), 1)
            block = jnp.where(lane < live, in_ref[c, :, aligned(t)].astype(F32), 0.0)
            out_ref[aligned(start + t), :] = block.T.astype(out_ref.dtype)
            return carry

        lax.fori_loop(0, offsets[c + 1] - start, body, 0)
    clear_tail(out_ref, offsets[clusters], out_ref.shape[0] // TILE)


def pack(tiles, counts, offsets, values):
    clusters, features, nodes = values.shape
    size = tiles * TILE * features
    return pl.pallas_call(
        functools.partial(pack_kernel, clusters),
        out_shape=jax.ShapeDtypeStruct((tiles * TILE, features), BF16),
        grid_spec=pltpu.PrefetchScalarGridSpec(
            num_scalar_prefetch=2,
            grid=(1,),
            in_specs=[pl.BlockSpec((clusters, features, nodes), lambda i, *_: (0, 0, 0))],
            out_specs=pl.BlockSpec((tiles * TILE, features), lambda i, *_: (0, 0)),
        ),
        compiler_params=params(),
        cost_estimate=cost(size, 4 * size),
    )(counts, offsets, values)


def unpack_kernel(counts, offsets, in_ref, out_ref):
    c = pl.program_id(0)
    features = out_ref.shape[1]
    live = counts[c]
    start = offsets[c]

    def body(t, carry):
        lane = t * TILE + lax.broadcasted_iota(jnp.int32, (features, TILE), 1)
        block = in_ref[aligned(start + t), :].astype(F32).T
        out_ref[0, :, aligned(t)] = jnp.where(lane < live, block, 0.0)
        return carry

    def clear(t, carry):
        out_ref[0, :, aligned(t)] = jnp.zeros((features, TILE), F32)
        return carry

    used = offsets[c + 1] - start
    lax.fori_loop(0, used, body, 0)
    lax.fori_loop(used, out_ref.shape[2] // TILE, clear, 0)


def unpack(shape, counts, offsets, packed):
    clusters, features, nodes = shape
    return pl.pallas_call(
        unpack_kernel,
        out_shape=jax.ShapeDtypeStruct(shape, F32),
        grid_spec=pltpu.PrefetchScalarGridSpec(
            num_scalar_prefetch=2,
            grid=(clusters,),
            in_specs=[pl.BlockSpec(packed.shape, lambda c, *_: (0, 0))],
            out_specs=pl.BlockSpec((1, features, nodes), lambda c, *_: (c, 0, 0)),
        ),
        compiler_params=params(),
        cost_estimate=cost(packed.size, 2 * packed.size + 4 * clusters * features * nodes),
    )(counts, offsets, packed)


def adjacency_spec(nodes):
    def index(c, i, counts, offsets):
        return (c, jnp.minimum(i, (counts[c] - 1) // ROWS), 0)

    return pl.BlockSpec((1, ROWS, nodes), index)


def aggregate_kernel(clusters, counts, offsets, x_ref, a_ref, out_ref, masked):
    c = pl.program_id(0)
    i = pl.program_id(1)
    live = counts[c]

    @pl.when(jnp.logical_and(c == 0, i == 0))
    def _():
        clear_tail(out_ref, offsets[clusters], out_ref.shape[0] // TILE)

    @pl.when(i == 0)
    def _():
        lane = lax.broadcasted_iota(jnp.int32, masked.shape, 1)
        masked[...] = jnp.where(lane < live, x_ref[0].astype(F32), 0.0).astype(BF16)

    @pl.when(i * ROWS < live)
    def _():
        total = dot(a_ref[0], masked[...], 1, 1)
        for s in range(ROWS // TILE):
            t = i * (ROWS // TILE) + s

            @pl.when(t * TILE < live)
            def _():
                block = a_ref[0, s * TILE : (s + 1) * TILE, aligned(t)]
                block = jnp.where(eye(), block.astype(F32), 0.0).astype(BF16)
                extra = dot(block, masked[:, aligned(t)], 1, 1)
                rows = total[s * TILE : (s + 1) * TILE] + extra
                out_ref[aligned(offsets[c] + t), :] = rows.astype(BF16)


def aggregate(tiles, counts, offsets, features, adjacency):
    clusters, width, nodes = features.shape
    return pl.pallas_call(
        functools.partial(aggregate_kernel, clusters),
        out_shape=jax.ShapeDtypeStruct((tiles * TILE, width), BF16),
        grid_spec=pltpu.PrefetchScalarGridSpec(
            num_scalar_prefetch=2,
            grid=(clusters, nodes // ROWS),
            in_specs=[
                pl.BlockSpec((1, width, nodes), lambda c, i, *_: (c, 0, 0)),
                adjacency_spec(nodes),
            ],
            out_specs=pl.BlockSpec((tiles * TILE, width), lambda c, i, *_: (0, 0)),
            scratch_shapes=[pltpu.VMEM((width, nodes), BF16)],
        ),
        compiler_params=params(),
        cost_estimate=cost(2 * adjacency.size * width, 2 * adjacency.size),
    )(counts, offsets, features, adjacency)


def spread_kernel(counts, offsets, g_ref, a_ref, out_ref, turned):
    c = pl.program_id(0)
    i = pl.program_id(1)
    live = counts[c]
    width = out_ref.shape[1]

    @pl.when(i == 0)
    def _():
        out_ref[...] = jnp.zeros_like(out_ref)

    @pl.when(i * ROWS < live)
    def _():
        for s in range(ROWS // TILE):
            t = i * (ROWS // TILE) + s
            place = jnp.minimum(offsets[c] + t, g_ref.shape[0] // TILE - 1)
            lane = t * TILE + lax.broadcasted_iota(jnp.int32, (width, TILE), 1)
            block = g_ref[aligned(place), :].astype(F32).T
            turned[:, s * TILE : (s + 1) * TILE] = jnp.where(lane < live, block, 0.0).astype(BF16)
        out_ref[0] += dot(turned[...], a_ref[0], 1, 0)
        for s in range(ROWS // TILE):
            t = i * (ROWS // TILE) + s
            block = a_ref[0, s * TILE : (s + 1) * TILE, aligned(t)]
            block = jnp.where(eye(), block.astype(F32), 0.0).astype(BF16)
            extra = dot(turned[:, s * TILE : (s + 1) * TILE], block, 1, 0)
            out_ref[0, :, aligned(t)] += extra

    @pl.when(i == pl.num_programs(1) - 1)
    def _():
        lane = lax.broadcasted_iota(jnp.int32, out_ref.shape[1:], 1)
        out_ref[0] = jnp.where(lane < live, out_ref[0], 0.0)


def spread(counts, offsets, packed, adjacency):
    clusters, nodes, _ = adjacency.shape
    width = packed.shape[1]
    return pl.pallas_call(
        spread_kernel,
        out_shape=jax.ShapeDtypeStruct((clusters, width, nodes), F32),
        grid_spec=pltpu.PrefetchScalarGridSpec(
            num_scalar_prefetch=2,
            grid=(clusters, nodes // ROWS),
            in_specs=[
                pl.BlockSpec(packed.shape, lambda c, i, *_: (0, 0)),
                adjacency_spec(nodes),
            ],
            out_specs=pl.BlockSpec((1, width, nodes), lambda c, i, *_: (c, 0, 0)),
            scratch_shapes=[pltpu.VMEM((width, ROWS), BF16)],
        ),
        compiler_params=params(),
        cost_estimate=cost(2 * adjacency.size * width, 2 * adjacency.size),
    )(counts, offsets, packed, adjacency)


def middle_kernel(agg_ref, cot_ref, w_ref, b_ref, act_ref, low_ref, bias_ref, held):
    owners, _, width = agg_ref.shape

    @pl.when(pl.program_id(0) == 0)
    def _():
        for s in range(owners):
            held[:, s * width : (s + 1) * width] = agg_ref[s]

    pre = dot(held[...], w_ref[...], 1, 0) + b_ref[...].astype(F32)
    parts = cot_ref.shape[0]
    cot = jnp.concatenate([cot_ref[k] for k in range(parts)], axis=1).astype(F32)
    cdf = 0.5 + 0.5 * lax.erf(pre * (0.5**0.5))
    pdf = jnp.exp(-0.5 * pre * pre) * 0.3989422804014327
    act = (pre * cdf).astype(BF16)
    grad = cot * (cdf + pre * pdf)
    for k in range(parts):
        act_ref[k] = act[:, k * width : (k + 1) * width]
    low_ref[...] = grad.astype(BF16)
    bias_ref[...] = jnp.sum(grad, axis=0, keepdims=True)


def middle(agg, cot, weight, bias):
    owners, rows, width = agg.shape
    full = owners * width
    block = 256
    return pl.pallas_call(
        middle_kernel,
        out_shape=(
            jax.ShapeDtypeStruct((owners, rows, width), BF16),
            jax.ShapeDtypeStruct((rows, full), BF16),
            jax.ShapeDtypeStruct((1, full), F32),
        ),
        grid=(full // block,),
        in_specs=[
            pl.BlockSpec((owners, rows, width), lambda g: (0, 0, 0)),
            pl.BlockSpec((block // width, rows, width), lambda g: (g, 0, 0)),
            pl.BlockSpec((full, block), lambda g: (0, g)),
            pl.BlockSpec((1, block), lambda g: (0, g)),
        ],
        out_specs=(
            pl.BlockSpec((block // width, rows, width), lambda g: (g, 0, 0)),
            pl.BlockSpec((rows, block), lambda g: (0, g)),
            pl.BlockSpec((1, block), lambda g: (0, g)),
        ),
        scratch_shapes=[pltpu.VMEM((rows, full), BF16)],
        compiler_params=params(),
        cost_estimate=cost(2 * rows * full * full, 2 * full * full + 8 * rows * full, 2 * rows * full),
    )(agg, cot, weight, bias[None])


def outer_kernel(which, agg_ref, low_ref, out_ref):
    left = jnp.concatenate([agg_ref[s] for s in range(agg_ref.shape[0])], axis=1)
    out_ref[...] = dot(left, low_ref[...], 0, 0).astype(out_ref.dtype)


def outer(which, count, agg, low, dtype):
    owners, rows, width = agg.shape
    full = owners * width
    part = full // count
    step = min(part, 256)
    steps = part // step
    return pl.pallas_call(
        outer_kernel,
        out_shape=jax.ShapeDtypeStruct((part, full), dtype),
        grid_spec=pltpu.PrefetchScalarGridSpec(
            num_scalar_prefetch=1,
            grid=(steps,),
            in_specs=[
                pl.BlockSpec((step // width, rows, width), lambda i, which: (which[0] * steps + i, 0, 0)),
                pl.BlockSpec((rows, full), lambda i, which: (0, 0)),
            ],
            out_specs=pl.BlockSpec((step, full), lambda i, which: (i, 0)),
        ),
        compiler_params=params(),
        cost_estimate=cost(2 * rows * part * full, 4 * rows * full + 4 * part * full),
    )(which[None], agg, low)


def back_kernel(low_ref, w_ref, out_ref):
    width = out_ref.shape[2]
    value = dot(low_ref[...], w_ref[...], 1, 1).astype(BF16)
    for s in range(out_ref.shape[0]):
        out_ref[s] = value[:, s * width : (s + 1) * width]


def back(low, weight, owners):
    rows, full = low.shape
    width = full // owners
    step = 256
    return pl.pallas_call(
        back_kernel,
        out_shape=jax.ShapeDtypeStruct((owners, rows, width), BF16),
        grid=(full // step,),
        in_specs=[
            pl.BlockSpec((rows, full), lambda i: (0, 0)),
            pl.BlockSpec((step, full), lambda i: (i, 0)),
        ],
        out_specs=pl.BlockSpec((step // width, rows, width), lambda i: (i, 0, 0)),
        compiler_params=params(),
        cost_estimate=cost(2 * rows * full * full, 2 * full * full + 4 * rows * full),
    )(low, weight)


def swap_feat(value, bit):
    count = lax.axis_size("feat")
    return lax.ppermute(value, "feat", [(i, i ^ (1 << bit)) for i in range(count)])


def swap_rep(value):
    return lax.ppermute(value, "rep", [(0, 1), (1, 0)])


def joined(mine, own, other):
    first = mine == 0
    return jnp.concatenate([jnp.where(first, own, other), jnp.where(first, other, own)], axis=0)


def exchange(packed):
    owners = lax.axis_size("feat")
    blocks = packed.reshape(owners, -1, packed.shape[-1])
    return lax.all_to_all(blocks, "feat", split_axis=0, concat_axis=0, tiled=True)


def weight_sum(agg, low, bias_part):
    me = lax.axis_index("feat")
    core = lax.axis_index("rep")
    bits = lax.axis_size("feat").bit_length() - 1
    orders = [list(range(bits)), [1, 0] + list(range(2, bits))]
    chunks = len(orders)
    bias_part = bias_part + swap_rep(bias_part)
    sent = [
        swap_rep(outer((1 - core) * chunks + k, 2 * chunks, agg, low, BF16)) for k in range(chunks)
    ]
    sums = [
        outer(core * chunks + k, 2 * chunks, agg, low, F32) + sent[k].astype(F32)
        for k in range(chunks)
    ]
    for stage in range(bits):
        bias_part = bias_part + swap_feat(bias_part, stage)
        for k in range(chunks):
            bit = orders[k][stage]
            mine = (me >> bit) & 1
            half = sums[k].shape[0] // 2
            away = lax.dynamic_slice_in_dim(sums[k], (1 - mine) * half, half, 0).astype(BF16)
            kept = lax.dynamic_slice_in_dim(sums[k], mine * half, half, 0)
            sums[k] = kept + swap_feat(away, bit).astype(F32)
    owned = [value.astype(BF16) for value in sums]
    for stage in reversed(range(bits)):
        for k in range(chunks):
            bit = orders[k][stage]
            owned[k] = joined((me >> bit) & 1, owned[k], swap_feat(owned[k], bit))
    other = [swap_rep(value) for value in owned]
    own = jnp.concatenate(owned, axis=0)
    other = jnp.concatenate(other, axis=0)
    return joined(core, own, other).astype(F32), bias_part[0]


def run(tiles, features, adjacency, counts, offsets, weight, bias, cotangent):
    owners = lax.axis_size("feat")
    cot = exchange(pack(tiles, counts, offsets, cotangent))
    agg = exchange(aggregate(tiles, counts, offsets, features, adjacency))
    act, low, bias_part = middle(agg, cot, weight, bias)
    act = exchange(act).reshape(tiles * TILE, -1)
    grad_rows = exchange(back(low, weight, owners)).reshape(tiles * TILE, -1)
    grad_weight, grad_bias = weight_sum(agg, low, bias_part)
    activations = unpack(features.shape, counts, offsets, act)
    grad_features = spread(counts, offsets, grad_rows, adjacency)
    return activations, grad_features, grad_weight, grad_bias


def local(features, adjacency, counts, weight, bias, cotangent):
    features = features.transpose(1, 0, 2)
    cotangent = cotangent.transpose(1, 0, 2)
    clusters, _, nodes = features.shape
    used = (counts + TILE - 1) // TILE
    before = jnp.arange(clusters)[None] < jnp.arange(clusters + 1)[:, None]
    offsets = jnp.sum(jnp.where(before, used[None], 0), axis=1).astype(jnp.int32)
    need = offsets[-1:]
    need = jnp.maximum(need, swap_rep(need))[0]
    most = clusters * nodes // TILE
    buckets = [b for b in BUCKETS if b < most] + [most]
    branch = sum([(need > b).astype(jnp.int32) for b in buckets[:-1]], jnp.int32(0))
    branches = [functools.partial(run, b) for b in buckets]
    args = (features, adjacency, counts, offsets, weight, bias, cotangent)
    activations, grad_features, grad_weight, grad_bias = lax.switch(branch, branches, *args)
    return (
        activations.transpose(1, 0, 2),
        grad_features.transpose(1, 0, 2),
        grad_weight,
        grad_bias,
    )


def solution(mesh):
    placed = (
        P("feat", "rep", None),
        P("rep", None, None),
        P("rep"),
        P(),
        P(),
        P("feat", "rep", None),
    )
    return jax.shard_map(
        local,
        mesh=mesh,
        in_specs=placed,
        out_specs=(P("feat", "rep", None), P("feat", "rep", None), P(), P()),
        check_vma=False,
    )
```

```python
import functools

import jax
import jax.numpy as jnp
from jax import lax
from jax.experimental import pallas as pl
from jax.experimental.pallas import tpu as pltpu
from jax.sharding import PartitionSpec as P

TILE = 128
ROWS = 512
SIDE = 512
OUTER = 4
CHUNKS = 2
F32 = jnp.float32
BF16 = jnp.bfloat16
BUCKETS = (60, 52, 56, 64, 68, 72)


def params(mib=60):
    return pltpu.CompilerParams(vmem_limit_bytes=mib * 1024 * 1024)


def cost(flops, moved, transcendentals=0):
    return pl.CostEstimate(flops=flops, bytes_accessed=moved, transcendentals=transcendentals)


def dot(a, b, ca, cb):
    return lax.dot_general(a, b, (((ca,), (cb,)), ((), ())), preferred_element_type=F32)


def anywhere(values):
    return [pl.BlockSpec(memory_space=pl.ANY) for _ in values]


def eye():
    row = lax.broadcasted_iota(jnp.int32, (TILE, TILE), 0)
    return row == lax.broadcasted_iota(jnp.int32, (TILE, TILE), 1)


def aligned(index, size=TILE):
    return pl.ds(pl.multiple_of(index * TILE, TILE), size)


def by_groups(first, last, one, size=4):
    groups = (last - first) // size

    def group(n, carry):
        for k in range(size):
            one(first + n * size + k)
        return carry

    def single(t, carry):
        one(t)
        return carry

    lax.fori_loop(0, groups, group, 0)
    lax.fori_loop(first + groups * size, last, single, 0)


def clear_tail(out_ref, first, last):
    def one(p):
        out_ref[aligned(p), :] = jnp.zeros((TILE, out_ref.shape[1]), out_ref.dtype)

    by_groups(first, last, one)


def pack_kernel(clusters, counts, offsets, in_ref, out_ref):
    features = in_ref.shape[1]
    for c in range(clusters):
        live = counts[c]
        start = offsets[c]

        def one(t):
            lane = t * TILE + lax.broadcasted_iota(jnp.int32, (features, TILE), 1)
            block = jnp.where(lane < live, in_ref[c, :, aligned(t)].astype(F32), 0.0)
            out_ref[aligned(start + t), :] = block.T.astype(out_ref.dtype)

        by_groups(0, offsets[c + 1] - start, one)
    clear_tail(out_ref, offsets[clusters], out_ref.shape[0] // TILE)


def pack(tiles, counts, offsets, values):
    clusters, features, nodes = values.shape
    size = tiles * TILE * features
    return pl.pallas_call(
        functools.partial(pack_kernel, clusters),
        name="pack",
        out_shape=jax.ShapeDtypeStruct((tiles * TILE, features), BF16),
        grid_spec=pltpu.PrefetchScalarGridSpec(
            num_scalar_prefetch=2,
            grid=(1,),
            in_specs=[pl.BlockSpec((clusters, features, nodes), lambda i, *_: (0, 0, 0))],
            out_specs=pl.BlockSpec((tiles * TILE, features), lambda i, *_: (0, 0)),
        ),
        compiler_params=params(),
        cost_estimate=cost(size, 4 * size),
    )(counts, offsets, values)


def unpack_kernel(counts, offsets, packed, *refs):
    out_ref = refs[-1]
    c = pl.program_id(0)
    features = out_ref.shape[1]
    live = counts[c]
    start = offsets[c]

    def one(t):
        lane = t * TILE + lax.broadcasted_iota(jnp.int32, (features, TILE), 1)
        block = packed[aligned(start + t), :].astype(F32).T
        out_ref[0, :, aligned(t)] = jnp.where(lane < live, block, 0.0)

    def clear(t):
        out_ref[0, :, aligned(t)] = jnp.zeros((features, TILE), F32)

    used = offsets[c + 1] - start
    by_groups(0, used, one)
    by_groups(used, out_ref.shape[2] // TILE, clear)


def unpack(shape, counts, offsets, packed, after=()):
    clusters, features, nodes = shape
    return pl.pallas_call(
        unpack_kernel,
        name="unpack",
        out_shape=jax.ShapeDtypeStruct(shape, F32),
        grid_spec=pltpu.PrefetchScalarGridSpec(
            num_scalar_prefetch=2,
            grid=(clusters,),
            in_specs=[pl.BlockSpec(packed.shape, lambda c, *_: (0, 0))] + anywhere(after),
            out_specs=pl.BlockSpec((1, features, nodes), lambda c, *_: (c, 0, 0)),
        ),
        compiler_params=params(),
        cost_estimate=cost(packed.size, 2 * packed.size + 4 * clusters * features * nodes),
    )(counts, offsets, packed, *after)


def adjacency_spec(nodes):
    def index(c, i, counts, offsets):
        return (c, jnp.minimum(i, (counts[c] - 1) // ROWS), 0)

    return pl.BlockSpec((1, ROWS, nodes), index)


def aggregate_kernel(clusters, counts, offsets, x_ref, a_ref, *refs):
    out_ref, masked = refs[-2:]
    c = pl.program_id(0)
    i = pl.program_id(1)
    live = counts[c]

    @pl.when(jnp.logical_and(c == 0, i == 0))
    def _():
        clear_tail(out_ref, offsets[clusters], out_ref.shape[0] // TILE)

    @pl.when(i == 0)
    def _():
        lane = lax.broadcasted_iota(jnp.int32, masked.shape, 1)
        masked[...] = jnp.where(lane < live, x_ref[0].astype(F32), 0.0).astype(BF16)

    @pl.when(i * ROWS < live)
    def _():
        total = dot(a_ref[0], masked[...], 1, 1)
        for s in range(ROWS // TILE):
            t = i * (ROWS // TILE) + s

            @pl.when(t * TILE < live)
            def _():
                block = a_ref[0, s * TILE : (s + 1) * TILE, aligned(t)]
                block = jnp.where(eye(), block.astype(F32), 0.0).astype(BF16)
                extra = dot(block, masked[:, aligned(t)], 1, 1)
                rows = total[s * TILE : (s + 1) * TILE] + extra
                out_ref[aligned(offsets[c] + t), :] = rows.astype(BF16)


def aggregate(tiles, counts, offsets, features, adjacency, after):
    clusters, width, nodes = features.shape
    return pl.pallas_call(
        functools.partial(aggregate_kernel, clusters),
        name="aggregate",
        out_shape=jax.ShapeDtypeStruct((tiles * TILE, width), BF16),
        grid_spec=pltpu.PrefetchScalarGridSpec(
            num_scalar_prefetch=2,
            grid=(clusters, nodes // ROWS),
            in_specs=[
                pl.BlockSpec((1, width, nodes), lambda c, i, *_: (c, 0, 0)),
                adjacency_spec(nodes),
                *anywhere((after,)),
            ],
            out_specs=pl.BlockSpec((tiles * TILE, width), lambda c, i, *_: (0, 0)),
            scratch_shapes=[pltpu.VMEM((width, nodes), BF16)],
        ),
        compiler_params=params(),
        cost_estimate=cost(2 * adjacency.size * width, 2 * adjacency.size),
    )(counts, offsets, features, adjacency, after)


def spread_kernel(clusters, count, counts, offsets, me, *refs):
    a_ref = refs[count]
    out_ref, packed, turned, held, sems = refs[-5:]
    c = pl.program_id(0)
    slot = lax.rem(c, 2)
    live = counts[c]
    width, nodes = turned.shape
    sizes = range(SIDE, nodes + SIDE, SIDE)

    def each(cluster, act):
        need = counts[cluster]
        for size in sizes:

            @pl.when(jnp.logical_and(need > size - SIDE, need <= size))
            def _():
                act(size)

    def copy(cluster, place, size):
        area = (slice(0, size), slice(0, size))
        return pltpu.make_async_copy(
            a_ref.at[(cluster, *area)], held.at[(place, *area)], sems.at[place]
        )

    @pl.when(c == 0)
    def _():
        each(c, lambda size: copy(c, slot, size).start())
        blocks = [(k, low, refs[low].at[k]) for low in range(count) for k in range(OUTER)]
        gather_rows(me[0], count, blocks, packed)

    @pl.when(c + 1 < clusters)
    def _():
        each(c + 1, lambda size: copy(c + 1, 1 - slot, size).start())

    start = offsets[c]
    used = offsets[c + 1] - start

    def turn(t):
        lane = t * TILE + lax.broadcasted_iota(jnp.int32, (width, TILE), 1)
        block = packed[aligned(start + t), :].astype(F32).T
        turned[:, aligned(t)] = jnp.where(lane < live, block, 0.0).astype(BF16)

    def clear(t):
        turned[:, aligned(t)] = jnp.zeros((width, TILE), BF16)

    by_groups(0, used, turn)
    by_groups(used, nodes // TILE, clear)

    def compute(size):
        copy(c, slot, size).wait()
        for j in range(0, size, SIDE):
            total = dot(turned[:, :size], held[slot, :size, j : j + SIDE], 1, 0)
            for t in range(j, j + SIDE, TILE):
                block = held[slot, t : t + TILE, t : t + TILE].astype(F32)
                diagonal = jnp.sum(jnp.where(eye(), block, 0.0), axis=0, keepdims=True)
                extra = diagonal * turned[:, t : t + TILE].astype(F32)
                lane = t + lax.broadcasted_iota(jnp.int32, (width, TILE), 1)
                value = total[:, t - j : t - j + TILE] + extra
                out_ref[0, :, t : t + TILE] = jnp.where(lane < live, value, 0.0)
        if size < nodes:
            out_ref[0, :, size:] = jnp.zeros((width, nodes - size), F32)

    each(c, compute)


def spread(counts, offsets, me, values, adjacency, after=()):
    clusters, nodes, _ = adjacency.shape
    count = len(values)
    width = values[0].shape[-1]
    return pl.pallas_call(
        functools.partial(spread_kernel, clusters, count),
        name="spread",
        out_shape=jax.ShapeDtypeStruct((clusters, width, nodes), F32),
        grid_spec=pltpu.PrefetchScalarGridSpec(
            num_scalar_prefetch=3,
            grid=(clusters,),
            in_specs=[pl.BlockSpec(values[0].shape, lambda c, *_: (0, 0, 0))] * count
            + anywhere((adjacency, *after)),
            out_specs=pl.BlockSpec((1, width, nodes), lambda c, *_: (c, 0, 0)),
            scratch_shapes=[
                pltpu.VMEM((count * values[0].size // width, width), BF16),
                pltpu.VMEM((width, nodes), BF16),
                pltpu.VMEM((2, nodes, nodes), BF16),
                pltpu.SemaphoreType.DMA((2,)),
            ],
        ),
        compiler_params=params(32),
        cost_estimate=cost(2 * adjacency.size * width, 2 * adjacency.size),
    )(counts, offsets, me, *values, adjacency, *after)


def normal(value):
    bell = jnp.exp(-0.5 * value * value)
    t = 1.0 / (1.0 + (0.3275911 * 0.5**0.5) * jnp.abs(value))
    tail = 0.5 * 1.061405429
    for term in (-1.453152027, 1.421413741, -0.284496736, 0.254829592):
        tail = tail * t + 0.5 * term
    tail = tail * t * bell
    return jnp.where(value >= 0.0, 1.0 - tail, tail), bell * 0.3989422804014327


def middle_kernel(first, which, *refs):
    refs = refs if first else refs[3:]
    agg_ref, cot_ref, w_ref, b_ref, act_ref, low_ref, bias_ref, *out_refs, held, turned = refs
    owners, rows, width = agg_ref.shape

    @pl.when(pl.program_id(0) == 0)
    def _():
        for s in range(owners):
            held[:, s * width : (s + 1) * width] = agg_ref[s]
            turned[s * width : (s + 1) * width, :] = agg_ref[s].T

    parts = cot_ref.shape[0]
    total = jnp.zeros((1, w_ref.shape[1]), F32)
    step = min(rows, TILE)
    for r in range(0, rows, step):
        pre = dot(held[r : r + step], w_ref[...], 1, 0) + b_ref[...].astype(F32)
        cdf, pdf = normal(pre)
        act = (pre * cdf).astype(BF16)
        cot = jnp.concatenate([cot_ref[k, r : r + step] for k in range(parts)], axis=1).astype(F32)
        grad = cot * (cdf + pre * pdf)
        for k in range(parts):
            act_ref[k, r : r + step] = act[:, k * width : (k + 1) * width]
        low_ref[r : r + step] = grad.astype(BF16)
        total = total + jnp.sum(grad, axis=0, keepdims=True)
    bias_ref[...] = total
    share = out_refs[0].shape[0]
    for k, out_ref in enumerate(out_refs):
        out_ref[...] = dot(turned[k * share : (k + 1) * share], low_ref[...], 1, 0).astype(out_ref.dtype)


def middle(which, dtype, agg, cot, weight, bias, before=None):
    owners, rows, width = agg.shape
    full = owners * width
    block = 256
    steps = full // 2 // block
    here = lambda g, which: (0, which[0] * steps + g)
    lead = lambda g, which: (which[0] * steps + g, 0, 0)
    begun = () if before is None else before
    return pl.pallas_call(
        functools.partial(middle_kernel, before is None),
        name="middle",
        out_shape=(
            jax.ShapeDtypeStruct((owners, rows, width), BF16),
            jax.ShapeDtypeStruct((rows, full), BF16),
            jax.ShapeDtypeStruct((1, full), F32),
        )
        + (jax.ShapeDtypeStruct((full // CHUNKS, full // 2), dtype),) * CHUNKS,
        grid_spec=pltpu.PrefetchScalarGridSpec(
            num_scalar_prefetch=1,
            grid=(steps,),
            in_specs=[pl.BlockSpec(memory_space=pl.ANY) for _ in begun]
            + [
                pl.BlockSpec((owners, rows, width), lambda g, which: (0, 0, 0)),
                pl.BlockSpec((block // width, rows, width), lead),
                pl.BlockSpec((full, block), here),
                pl.BlockSpec((1, block), here),
            ],
            out_specs=(
                pl.BlockSpec((block // width, rows, width), lead),
                pl.BlockSpec((rows, block), here),
                pl.BlockSpec((1, block), here),
            )
            + (pl.BlockSpec((full // CHUNKS, block), lambda g, which: (0, g)),) * CHUNKS,
            scratch_shapes=[pltpu.VMEM((rows, full), BF16), pltpu.VMEM((full, rows), BF16)],
        ),
        input_output_aliases={1 + k: k for k in range(len(begun))},
        compiler_params=params(),
        cost_estimate=cost(2 * rows * full * full, full * full + 8 * rows * full, rows * full),
    )(which[None], *begun, agg, cot, weight, bias[None])


def back_kernel(me, low_ref, w_ref, *refs):
    out_ref = refs[-1]
    parts, width = out_ref.shape[1], out_ref.shape[3]
    value = dot(low_ref[...], w_ref[...], 1, 1).astype(BF16)
    for k in range(parts):
        out_ref[0, k ^ (me[0] & (parts - 1))] = value[:, k * width : (k + 1) * width]


def back(me, low, weight, owners, after=()):
    rows, full = low.shape
    width = full // owners
    step = 256
    parts = step // width
    inner = owners // OUTER

    def place(i, me):
        rest = i ^ (me[0] // parts)
        return (i // (inner // parts), rest % (inner // parts), 0, 0)

    return pl.pallas_call(
        back_kernel,
        name="back",
        out_shape=jax.ShapeDtypeStruct((OUTER, inner, rows, width), BF16),
        grid_spec=pltpu.PrefetchScalarGridSpec(
            num_scalar_prefetch=1,
            grid=(full // step,),
            in_specs=[
                pl.BlockSpec((rows, full), lambda i, me: (0, 0)),
                pl.BlockSpec((step, full), lambda i, me: (i, 0)),
            ]
            + anywhere(after),
            out_specs=pl.BlockSpec((1, parts, rows, width), place),
        ),
        compiler_params=params(16),
        cost_estimate=cost(8 * rows * full * full, 8 * full * full + 16 * rows * full),
    )(me, low, weight, *after)


def split_kernel(value_ref, *refs):
    count = value_ref.shape[1]
    for j, out_ref in enumerate(refs[-count:]):
        out_ref[...] = value_ref[:, j]


def row_step(rows):
    return rows // 2 if rows % 32 == 0 else rows


def split(value, after=()):
    first, second, rows, width = value.shape
    step = row_step(rows)
    return pl.pallas_call(
        split_kernel,
        name="split",
        out_shape=[jax.ShapeDtypeStruct((first, rows, width), BF16)] * second,
        grid=(rows // step,),
        in_specs=[pl.BlockSpec((first, second, step, width), lambda i: (0, 0, i, 0))]
        + anywhere(after),
        out_specs=[pl.BlockSpec((first, step, width), lambda i: (0, i, 0))] * second,
        compiler_params=params(16),
        cost_estimate=cost(0, 4 * value.size),
    )(value, *after)


def swap_with(value, mask):
    count = lax.axis_size("feat")
    return lax.ppermute(value, "feat", [(i, i ^ mask) for i in range(count)])


def scatter(values):
    return [values[0]] + [swap_with(values[k], k) for k in range(1, len(values))]


def outer_exchange(value):
    inner = lax.axis_size("feat") // OUTER
    groups = [[k * inner + low for k in range(OUTER)] for low in range(inner)]
    return lax.all_to_all(
        value, "feat", split_axis=0, concat_axis=0, axis_index_groups=groups, tiled=True
    )


def gather_rows(me, inner, blocks, out_ref):
    for high, low, block in blocks:
        rows = block.shape[0]
        owner = high * inner + (me ^ low)
        out_ref[pl.ds(pl.multiple_of(owner * rows, 16), rows), :] = block[...]


def swap_feat(value, bit):
    return swap_with(value, 1 << bit)


def swap_rep(value):
    return lax.ppermute(value, "rep", [(0, 1), (1, 0)])


def exchange(packed):
    owners = lax.axis_size("feat")
    blocks = packed.reshape(owners, -1, packed.shape[-1])
    return lax.all_to_all(blocks, "feat", split_axis=0, concat_axis=0, tiled=True)


def place_kernel(count, where, *refs):
    out_ref = refs[-1]
    for k in range(count):

        @pl.when(pl.program_id(0) == k)
        def _():
            out_ref[...] = refs[k][...].astype(F32)


def place(where, pieces, before=None, after=()):
    count = len(pieces)
    rows, columns = pieces[0].shape
    step = min(rows, 512)
    steps = rows // step
    full = 2 * columns
    begun = () if before is None else (before,)

    def source(k):
        return lambda i, j, where: (jnp.where(i == k, j, jnp.where(i < k, 0, steps - 1)), 0)

    return pl.pallas_call(
        functools.partial(place_kernel, count),
        name="place",
        out_shape=jax.ShapeDtypeStruct((full, full), F32),
        grid_spec=pltpu.PrefetchScalarGridSpec(
            num_scalar_prefetch=1,
            grid=(count, steps),
            in_specs=[pl.BlockSpec((step, columns), source(k)) for k in range(count)]
            + anywhere(begun)
            + anywhere(after),
            out_specs=pl.BlockSpec(
                (step, columns), lambda i, j, where: (where[i] * steps + j, where[count + i])
            ),
        ),
        input_output_aliases={1 + count: 0} if begun else {},
        compiler_params=params(16),
        cost_estimate=cost(0, 6 * count * rows * columns),
    )(jnp.stack(where).astype(jnp.int32), *pieces, *begun, *after)


def halve_kernel(chunks, side, *refs):
    outs = refs[-2 * chunks :]
    for k in range(chunks):
        for part in range(2):
            kept, came = refs[4 * k + 2 * part], refs[4 * k + 2 * part + 1]
            out = outs[2 * k + part]
            out[...] = (kept[...].astype(F32) + came[...].astype(F32)).astype(out.dtype)


def halve(side, kept, came, after=()):
    chunks = len(kept)
    half, columns = kept[0].shape[0] // 2, kept[0].shape[1]
    step = min(half, 128)
    steps = half // step

    def source(k, part):
        return lambda i, side: ((side[k] if part else 1 - side[k]) * steps + i, 0)

    in_specs = []
    operands = []
    out_shape = []
    for k in range(chunks):
        for part in range(2):
            for value in (kept[k], came[k]):
                in_specs.append(pl.BlockSpec((step, columns), source(k, part)))
                operands.append(value)
        for dtype in (BF16, F32):
            out_shape.append(jax.ShapeDtypeStruct((half, columns), dtype))
    outs = pl.pallas_call(
        functools.partial(halve_kernel, chunks),
        name="halve",
        out_shape=tuple(out_shape),
        grid_spec=pltpu.PrefetchScalarGridSpec(
            num_scalar_prefetch=1,
            grid=(steps,),
            in_specs=in_specs + anywhere(after),
            out_specs=[pl.BlockSpec((step, columns), lambda i, side: (i, 0)) for _ in out_shape],
        ),
        compiler_params=params(16),
        cost_estimate=cost(2 * chunks * half * columns, 18 * chunks * half * columns),
    )(jnp.stack(side).astype(jnp.int32), *operands, *after)
    return outs[0::2], outs[1::2]


def pick_kernel(side, *refs):
    first, second = (refs[2 * k][...] + refs[2 * k + 1][...].astype(F32) for k in range(2))
    away_ref, own_ref = refs[-2:]

    @pl.when(side[0] == 0)
    def _():
        own_ref[...] = first
        away_ref[...] = second.astype(BF16)

    @pl.when(side[0] == 1)
    def _():
        own_ref[...] = second
        away_ref[...] = first.astype(BF16)


def pick(side, kept, came, after=()):
    rows, columns = kept[0].shape
    step = min(rows, 128)
    block = pl.BlockSpec((step, columns), lambda i, side: (i, 0))
    away, own = pl.pallas_call(
        pick_kernel,
        name="pick",
        out_shape=(
            jax.ShapeDtypeStruct((rows, columns), BF16),
            jax.ShapeDtypeStruct((rows, columns), F32),
        ),
        grid_spec=pltpu.PrefetchScalarGridSpec(
            num_scalar_prefetch=1,
            grid=(rows // step,),
            in_specs=[block] * 4 + anywhere(after),
            out_specs=(block, block),
        ),
        compiler_params=params(16),
        cost_estimate=cost(2 * rows * columns, 18 * rows * columns),
    )(side[None].astype(jnp.int32), kept[0], came[0], kept[1], came[1], *after)
    return [away], [own]


def sort_kernel(side, own_ref, other_ref, *refs):
    first_ref, second_ref = refs[-2:]

    @pl.when(side[0] == 0)
    def _():
        first_ref[...] = own_ref[...]
        second_ref[...] = other_ref[...]

    @pl.when(side[0] == 1)
    def _():
        first_ref[...] = other_ref[...]
        second_ref[...] = own_ref[...]


def sort(side, own, other, after=()):
    whole = pl.BlockSpec(own.shape, lambda i, side: (0, 0))
    return pl.pallas_call(
        sort_kernel,
        name="sort",
        out_shape=[jax.ShapeDtypeStruct(own.shape, BF16)] * 2,
        grid_spec=pltpu.PrefetchScalarGridSpec(
            num_scalar_prefetch=1,
            grid=(1,),
            in_specs=[whole, whole] + anywhere(after),
            out_specs=[whole, whole],
        ),
        compiler_params=params(16),
        cost_estimate=cost(0, 8 * own.size),
    )(side[None].astype(jnp.int32), own, other, *after)


def add_kernel(first_ref, second_ref, *refs):
    refs[-1][...] = first_ref[...] + second_ref[...]


def add(first, second, after=()):
    return pl.pallas_call(
        add_kernel,
        name="add",
        out_shape=jax.ShapeDtypeStruct(first.shape, F32),
        in_specs=[pl.BlockSpec(memory_space=pltpu.VMEM)] * 2 + anywhere(after),
        compiler_params=params(16),
        cost_estimate=cost(first.size, 12 * first.size),
    )(first, second, *after)


def close_kernel(chunks, *refs):
    for k in range(chunks):
        total = refs[2 * k][...] + refs[2 * k + 1][...].astype(F32)
        refs[len(refs) - chunks + k][...] = total.astype(BF16)


def close(kept, came, after=()):
    chunks = len(kept)
    pairs = [value for pair in zip(kept, came) for value in pair]
    return pl.pallas_call(
        functools.partial(close_kernel, chunks),
        name="close",
        out_shape=[jax.ShapeDtypeStruct(value.shape, BF16) for value in kept],
        in_specs=[pl.BlockSpec(memory_space=pltpu.VMEM) for _ in pairs] + anywhere(after),
        compiler_params=params(16),
        cost_estimate=cost(kept[0].size * chunks, 8 * kept[0].size * chunks),
    )(*pairs, *after)


def join_kernel(chunks, side, *refs):
    outs = refs[-chunks:]
    for k in range(chunks):
        for part in range(2):

            @pl.when(pl.program_id(0) == part)
            def _():
                outs[k][...] = refs[2 * k + part][...]


def join(side, own, other, after=()):
    chunks = len(own)
    rows, columns = own[0].shape
    step = min(rows, 256)
    steps = rows // step
    pairs = [value for pair in zip(own, other) for value in pair]

    def source(part):
        return lambda i, j, side: (jnp.where(i == part, j, 0 if part else steps - 1), 0)

    def target(k):
        return lambda i, j, side: (jnp.where(i == 0, side[k], 1 - side[k]) * steps + j, 0)

    return pl.pallas_call(
        functools.partial(join_kernel, chunks),
        name="join",
        out_shape=[jax.ShapeDtypeStruct((2 * rows, columns), BF16) for _ in own],
        grid_spec=pltpu.PrefetchScalarGridSpec(
            num_scalar_prefetch=1,
            grid=(2, steps),
            in_specs=[pl.BlockSpec((step, columns), source(n % 2)) for n in range(2 * chunks)]
            + anywhere(after),
            out_specs=[pl.BlockSpec((step, columns), target(k)) for k in range(chunks)],
        ),
        compiler_params=params(16),
        cost_estimate=cost(0, 8 * chunks * rows * columns),
    )(jnp.stack(side).astype(jnp.int32), *pairs, *after)


def run(tiles, features, adjacency, counts, offsets, weight, bias, cotangent):
    owners = lax.axis_size("feat")
    me = lax.axis_index("feat")
    core = lax.axis_index("rep")
    bits = owners.bit_length() - 1
    inner = owners // OUTER
    side = [(me >> bit) & 1 for bit in range(bits)]
    crossed = [1, 0]
    low_bits = (me & (inner - 1)).astype(jnp.int32)
    place_of = low_bits[None]

    cot = pack(tiles, counts, offsets, cotangent)
    agg = exchange(aggregate(tiles, counts, offsets, features, adjacency, cot))
    cot = exchange(cot)
    *begun, sent0, sent1 = middle(1 - core, BF16, agg, cot, weight, bias)
    came = [swap_rep(sent0), swap_rep(sent1)]
    act, low, grad_bias, *kept = middle(
        core, BF16, agg, cot, weight, bias, begun
    )

    came_bias = swap_rep(grad_bias)
    away, kept = halve(side[:2], kept, came)
    came = [swap_feat(away[k], k) for k in range(2)]
    back_rows = outer_exchange(back(place_of, low, weight, owners, away))
    grad_bias = add(grad_bias, came_bias, away)
    came_bias = swap_feat(grad_bias, 0)
    away, kept = halve([side[1], side[0]], kept, came)
    came = [swap_feat(away[k], crossed[k]) for k in range(2)]
    grad_bias = add(grad_bias, came_bias, away)
    came_bias = swap_feat(grad_bias, 1)
    away, kept = pick(side[2], kept, came, (grad_bias,))
    came = [swap_feat(away[0], 2)]
    back_rows = scatter(split(back_rows, away))
    grad_bias = add(grad_bias, came_bias, away)
    for bit in range(3, bits):
        came_bias = swap_feat(grad_bias, bit - 1)
        away, kept = halve(side[bit : bit + 1], kept, came, (grad_bias,))
        came = [swap_feat(away[0], bit)]
        grad_bias = add(grad_bias, came_bias, away)
    came_bias = swap_feat(grad_bias, bits - 1)
    grad_bias = add(grad_bias, came_bias, away)
    owned = close(kept, came, (grad_bias,))
    for bit in reversed(range(3, bits)):
        owned = join(side[bit : bit + 1], owned, [swap_feat(owned[0], bit)])
    other = swap_feat(owned[0], 2)
    grad_features = spread(counts, offsets, place_of, back_rows, adjacency, owned)
    owned = sort(side[2], owned[0], other, (grad_features,))
    other = [swap_feat(owned[k], crossed[k]) for k in range(2)]
    act, owned = lax.optimization_barrier((act, owned))
    act = exchange(act).reshape(tiles * TILE, -1)
    owned = join([side[1], side[0]], owned, other)
    across = [swap_rep(value) for value in owned]
    far = [swap_feat(owned[k], k) for k in range(2)]
    near_rows = [2 * k + side[k] for k in range(2)]
    far_rows = [2 * k + 1 - side[k] for k in range(2)]
    columns = [core] * 2 + [1 - core] * 2
    grad_weight = place(2 * near_rows + columns, [*owned, *across])
    far, grad_weight = lax.optimization_barrier((far, grad_weight))
    far_across = [swap_rep(value) for value in far]
    grad_weight = place(2 * far_rows + columns, [*far, *far_across], grad_weight)
    activations = unpack(features.shape, counts, offsets, act)
    return activations, grad_features, grad_weight, grad_bias[0]


def local(features, adjacency, counts, weight, bias, cotangent):
    features = features.transpose(1, 0, 2)
    cotangent = cotangent.transpose(1, 0, 2)
    clusters, _, nodes = features.shape
    used = (counts + TILE - 1) // TILE
    before = jnp.arange(clusters)[None] < jnp.arange(clusters + 1)[:, None]
    offsets = jnp.sum(jnp.where(before, used[None], 0), axis=1).astype(jnp.int32)
    need = offsets[-1:]
    need = jnp.maximum(need, swap_rep(need))[0]
    most = clusters * nodes // TILE
    unit = max(2, 16 * lax.axis_size("feat") // TILE)
    buckets = [b for b in BUCKETS if b < most and b % unit == 0] + [most]
    ordered = sorted(buckets)
    branch = jnp.int32(buckets.index(ordered[0]))
    for low, high in zip(ordered, ordered[1:]):
        branch = jnp.where(need > low, buckets.index(high), branch)
    branches = [functools.partial(run, b) for b in buckets]
    args = (features, adjacency, counts, offsets, weight, bias, cotangent)
    activations, grad_features, grad_weight, grad_bias = lax.switch(branch, branches, *args)
    return (
        activations.transpose(1, 0, 2),
        grad_features.transpose(1, 0, 2),
        grad_weight,
        grad_bias,
    )


def solution(mesh):
    placed = (
        P("feat", "rep", None),
        P("rep", None, None),
        P("rep"),
        P(),
        P(),
        P("feat", "rep", None),
    )
    return jax.shard_map(
        local,
        mesh=mesh,
        in_specs=placed,
        out_specs=(P("feat", "rep", None), P("feat", "rep", None), P(), P()),
        check_vma=False,
    )
```

```python
import functools

import jax
import jax.numpy as jnp
from jax import lax
from jax.experimental import pallas as pl
from jax.experimental.pallas import tpu as pltpu
from jax.sharding import PartitionSpec as P

TILE = 128
ROWS = 512
SIDE = 512
OUTER = 4
SLAB = 128
DEEP = 512
CHUNKS = 2
F32 = jnp.float32
BF16 = jnp.bfloat16
BUCKETS = (60, 52, 56, 64, 68, 72)


def params(mib=60):
    return pltpu.CompilerParams(vmem_limit_bytes=mib * 1024 * 1024)


def cost(flops, moved, transcendentals=0):
    return pl.CostEstimate(flops=flops, bytes_accessed=moved, transcendentals=transcendentals)


def dot(a, b, ca, cb):
    return lax.dot_general(a, b, (((ca,), (cb,)), ((), ())), preferred_element_type=F32)


def anywhere(values):
    return [pl.BlockSpec(memory_space=pl.ANY) for _ in values]


def eye():
    row = lax.broadcasted_iota(jnp.int32, (TILE, TILE), 0)
    return row == lax.broadcasted_iota(jnp.int32, (TILE, TILE), 1)


def aligned(index, size=TILE):
    return pl.ds(pl.multiple_of(index * TILE, TILE), size)


def by_groups(first, last, one, size=4):
    groups = (last - first) // size

    def group(n, carry):
        for k in range(size):
            one(first + n * size + k)
        return carry

    def single(t, carry):
        one(t)
        return carry

    lax.fori_loop(0, groups, group, 0)
    lax.fori_loop(first + groups * size, last, single, 0)


def clear_tail(out_ref, first, last):
    def one(p):
        out_ref[aligned(p), :] = jnp.zeros((TILE, out_ref.shape[1]), out_ref.dtype)

    by_groups(first, last, one)


def pack_kernel(clusters, counts, offsets, in_ref, out_ref):
    features = in_ref.shape[1]
    for c in range(clusters):
        live = counts[c]
        start = offsets[c]

        def one(t):
            lane = t * TILE + lax.broadcasted_iota(jnp.int32, (features, TILE), 1)
            block = jnp.where(lane < live, in_ref[c, :, aligned(t)].astype(F32), 0.0)
            out_ref[aligned(start + t), :] = block.T.astype(out_ref.dtype)

        by_groups(0, offsets[c + 1] - start, one)
    clear_tail(out_ref, offsets[clusters], out_ref.shape[0] // TILE)


def pack(tiles, counts, offsets, values):
    clusters, features, nodes = values.shape
    size = tiles * TILE * features
    return pl.pallas_call(
        functools.partial(pack_kernel, clusters),
        name="pack",
        out_shape=jax.ShapeDtypeStruct((tiles * TILE, features), BF16),
        grid_spec=pltpu.PrefetchScalarGridSpec(
            num_scalar_prefetch=2,
            grid=(1,),
            in_specs=[pl.BlockSpec((clusters, features, nodes), lambda i, *_: (0, 0, 0))],
            out_specs=pl.BlockSpec((tiles * TILE, features), lambda i, *_: (0, 0)),
        ),
        compiler_params=params(16),
        cost_estimate=cost(size, 4 * size),
    )(counts, offsets, values)


def unpack_kernel(count, counts, offsets, me, *refs):
    out_ref, packed = refs[-2:]
    c = pl.program_id(0)
    features = out_ref.shape[1]
    live = counts[c]
    start = offsets[c]

    @pl.when(c == 0)
    def _():
        blocks = [(k, low, refs[low].at[k]) for low in range(count) for k in range(OUTER)]
        gather_rows(me[0], count, blocks, packed)

    def one(t):
        lane = t * TILE + lax.broadcasted_iota(jnp.int32, (features, TILE), 1)
        block = packed[aligned(start + t), :].astype(F32).T
        out_ref[0, :, aligned(t)] = jnp.where(lane < live, block, 0.0)

    def clear(t):
        out_ref[0, :, aligned(t)] = jnp.zeros((features, TILE), F32)

    used = offsets[c + 1] - start
    by_groups(0, used, one)
    by_groups(used, out_ref.shape[2] // TILE, clear)


def unpack(shape, counts, offsets, me, values, after=()):
    clusters, features, nodes = shape
    count = len(values)
    size = count * values[0].size
    whole = pl.BlockSpec(values[0].shape, lambda c, *_: (0, 0, 0))
    return pl.pallas_call(
        functools.partial(unpack_kernel, count),
        name="unpack",
        out_shape=jax.ShapeDtypeStruct(shape, F32),
        grid_spec=pltpu.PrefetchScalarGridSpec(
            num_scalar_prefetch=3,
            grid=(clusters,),
            in_specs=[whole] * count + anywhere(after),
            out_specs=pl.BlockSpec((1, features, nodes), lambda c, *_: (c, 0, 0)),
            scratch_shapes=[pltpu.VMEM((size // features, features), BF16)],
        ),
        compiler_params=params(16),
        cost_estimate=cost(size, 2 * size + 4 * clusters * features * nodes),
    )(counts, offsets, me, *values, *after)


def adjacency_spec(nodes):
    def index(c, i, counts, offsets):
        return (c, jnp.minimum(i, (counts[c] - 1) // ROWS), 0)

    return pl.BlockSpec((1, ROWS, nodes), index)


def aggregate_kernel(clusters, counts, offsets, x_ref, a_ref, *refs):
    out_ref, masked = refs[-2:]
    c = pl.program_id(0)
    i = pl.program_id(1)
    live = counts[c]

    @pl.when(jnp.logical_and(c == 0, i == 0))
    def _():
        clear_tail(out_ref, offsets[clusters], out_ref.shape[0] // TILE)

    @pl.when(i == 0)
    def _():
        lane = lax.broadcasted_iota(jnp.int32, masked.shape, 1)
        masked[...] = jnp.where(lane < live, x_ref[0].astype(F32), 0.0).astype(BF16)

    @pl.when(i * ROWS < live)
    def _():
        total = dot(a_ref[0], masked[...], 1, 1)
        for s in range(ROWS // TILE):
            t = i * (ROWS // TILE) + s

            @pl.when(t * TILE < live)
            def _():
                block = a_ref[0, s * TILE : (s + 1) * TILE, aligned(t)]
                block = jnp.where(eye(), block.astype(F32), 0.0).astype(BF16)
                extra = dot(block, masked[:, aligned(t)], 1, 1)
                rows = total[s * TILE : (s + 1) * TILE] + extra
                out_ref[aligned(offsets[c] + t), :] = rows.astype(BF16)


def aggregate(tiles, counts, offsets, features, adjacency, after):
    clusters, width, nodes = features.shape
    return pl.pallas_call(
        functools.partial(aggregate_kernel, clusters),
        name="aggregate",
        out_shape=jax.ShapeDtypeStruct((tiles * TILE, width), BF16),
        grid_spec=pltpu.PrefetchScalarGridSpec(
            num_scalar_prefetch=2,
            grid=(clusters, nodes // ROWS),
            in_specs=[
                pl.BlockSpec((1, width, nodes), lambda c, i, *_: (c, 0, 0)),
                adjacency_spec(nodes),
                *anywhere((after,)),
            ],
            out_specs=pl.BlockSpec((tiles * TILE, width), lambda c, i, *_: (0, 0)),
            scratch_shapes=[pltpu.VMEM((width, nodes), BF16)],
        ),
        compiler_params=params(16),
        cost_estimate=cost(2 * adjacency.size * width, 2 * adjacency.size),
    )(counts, offsets, features, adjacency, after)


def spread_kernel(clusters, counts, offsets, packed, a_ref, *refs):
    out_ref, turned, held, sems = refs[-4:]
    c = pl.program_id(0)
    slot = lax.rem(c, 2)
    live = counts[c]
    width, nodes = turned.shape
    sizes = range(SIDE, nodes + SIDE, SIDE)

    def each(cluster, act):
        need = counts[cluster]
        for size in sizes:

            @pl.when(jnp.logical_and(need > size - SIDE, need <= size))
            def _():
                act(size)

    def copy(cluster, place, size):
        area = (slice(0, size), slice(0, size))
        return pltpu.make_async_copy(
            a_ref.at[(cluster, *area)], held.at[(place, *area)], sems.at[place]
        )

    @pl.when(c == 0)
    def _():
        each(c, lambda size: copy(c, slot, size).start())

    @pl.when(c + 1 < clusters)
    def _():
        each(c + 1, lambda size: copy(c + 1, 1 - slot, size).start())

    start = offsets[c]
    used = offsets[c + 1] - start

    def turn(t):
        lane = t * TILE + lax.broadcasted_iota(jnp.int32, (width, TILE), 1)
        block = packed[aligned(start + t), :].astype(F32).T
        turned[:, aligned(t)] = jnp.where(lane < live, block, 0.0).astype(BF16)

    def clear(t):
        turned[:, aligned(t)] = jnp.zeros((width, TILE), BF16)

    by_groups(0, used, turn)
    by_groups(used, nodes // TILE, clear)

    def compute(size):
        copy(c, slot, size).wait()
        for j in range(0, size, SIDE):
            total = dot(turned[:, :size], held[slot, :size, j : j + SIDE], 1, 0)
            for t in range(j, j + SIDE, TILE):
                block = held[slot, t : t + TILE, t : t + TILE].astype(F32)
                diagonal = jnp.sum(jnp.where(eye(), block, 0.0), axis=0, keepdims=True)
                extra = diagonal * turned[:, t : t + TILE].astype(F32)
                lane = t + lax.broadcasted_iota(jnp.int32, (width, TILE), 1)
                value = total[:, t - j : t - j + TILE] + extra
                out_ref[0, :, t : t + TILE] = jnp.where(lane < live, value, 0.0)
        if size < nodes:
            out_ref[0, :, size:] = jnp.zeros((width, nodes - size), F32)

    each(c, compute)


def spread(counts, offsets, packed, adjacency, after=()):
    clusters, nodes, _ = adjacency.shape
    width = packed.shape[1]
    return pl.pallas_call(
        functools.partial(spread_kernel, clusters),
        name="spread",
        out_shape=jax.ShapeDtypeStruct((clusters, width, nodes), F32),
        grid_spec=pltpu.PrefetchScalarGridSpec(
            num_scalar_prefetch=2,
            grid=(clusters,),
            in_specs=[pl.BlockSpec(packed.shape, lambda c, *_: (0, 0))]
            + anywhere((adjacency, *after)),
            out_specs=pl.BlockSpec((1, width, nodes), lambda c, *_: (c, 0, 0)),
            scratch_shapes=[
                pltpu.VMEM((width, nodes), BF16),
                pltpu.VMEM((2, nodes, nodes), BF16),
                pltpu.SemaphoreType.DMA((2,)),
            ],
        ),
        compiler_params=params(32),
        cost_estimate=cost(2 * adjacency.size * width, 2 * adjacency.size),
    )(counts, offsets, packed, adjacency, *after)


def normal(value):
    bell = jnp.exp(-0.5 * value * value)
    t = 1.0 / (1.0 + (0.3275911 * 0.5**0.5) * jnp.abs(value))
    tail = 0.5 * 1.061405429
    for term in (-1.453152027, 1.421413741, -0.284496736, 0.254829592):
        tail = tail * t + 0.5 * term
    tail = tail * t * bell
    return jnp.where(value >= 0.0, 1.0 - tail, tail), bell * 0.3989422804014327


def middle_kernel(me, agg_ref, cot_ref, w_ref, b_ref, act_ref, low_ref, bias_ref, held, product):
    owners, rows, width = agg_ref.shape

    @pl.when(pl.program_id(0) == 0)
    def _():
        for s in range(owners):
            held[:, s * width : (s + 1) * width] = agg_ref[s]

    parts = cot_ref.shape[0]
    total = jnp.zeros((1, w_ref.shape[1]), F32)
    product[...] = dot(held[...], w_ref[...], 1, 0)
    step = SLAB
    for r in range(0, rows, step):
        pre = product[r : r + step] + b_ref[...].astype(F32)
        cdf, pdf = normal(pre)
        act = (pre * cdf).astype(BF16)
        cot = jnp.concatenate([cot_ref[k, r : r + step] for k in range(parts)], axis=1).astype(F32)
        grad = cot * (cdf + pre * pdf)
        for k in range(parts):
            act_ref[0, k ^ me[0], r : r + step] = act[:, k * width : (k + 1) * width]
        low_ref[r : r + step] = grad.astype(BF16)
        total = total + jnp.sum(grad, axis=0, keepdims=True)
    bias_ref[...] = total


def middle(me, agg, cot, weight, bias):
    owners, rows, width = agg.shape
    full = owners * width
    inner = owners // OUTER
    block = inner * width
    return pl.pallas_call(
        middle_kernel,
        name="middle",
        out_shape=(
            jax.ShapeDtypeStruct((OUTER, inner, rows, width), BF16),
            jax.ShapeDtypeStruct((rows, full), BF16),
            jax.ShapeDtypeStruct((1, full), F32),
        ),
        grid_spec=pltpu.PrefetchScalarGridSpec(
            num_scalar_prefetch=1,
            grid=(OUTER,),
            in_specs=[
                pl.BlockSpec((owners, rows, width), lambda g, me: (0, 0, 0)),
                pl.BlockSpec((inner, rows, width), lambda g, me: (g, 0, 0)),
                pl.BlockSpec((full, block), lambda g, me: (0, g)),
                pl.BlockSpec((1, block), lambda g, me: (0, g)),
            ],
            out_specs=(
                pl.BlockSpec((1, inner, rows, width), lambda g, me: (g, 0, 0, 0)),
                pl.BlockSpec((rows, block), lambda g, me: (0, g)),
                pl.BlockSpec((1, block), lambda g, me: (0, g)),
            ),
            scratch_shapes=[pltpu.VMEM((rows, full), BF16), pltpu.VMEM((rows, block), F32)],
        ),
        compiler_params=params(28),
        cost_estimate=cost(2 * rows * full * full, 2 * full * full + 8 * rows * full),
    )(me, agg, cot, weight, bias[None])


def turned_dot(agg_ref, low_ref):
    left = jnp.concatenate([agg_ref[s].T for s in range(agg_ref.shape[0])], axis=0)
    return dot(left, low_ref[...], 1, 0)


def clamped(i, first, count):
    return jnp.clip(i - first, 0, count - 1)


def outer_kernel(blocks, which, agg_ref, low_ref, *out_refs):
    for k, out_ref in enumerate(out_refs):

        @pl.when(pl.program_id(0) // blocks == k)
        def _():
            out_ref[...] = turned_dot(agg_ref, low_ref).astype(BF16)


def outer(which, agg, low):
    owners, rows, width = agg.shape
    full = owners * width
    step = DEEP
    share = full // CHUNKS
    blocks = share // step

    def target(k):
        return lambda i, which: (clamped(i, k * blocks, blocks), 0)

    return pl.pallas_call(
        functools.partial(outer_kernel, blocks),
        name="outer",
        out_shape=[jax.ShapeDtypeStruct((share, full // 2), BF16)] * CHUNKS,
        grid_spec=pltpu.PrefetchScalarGridSpec(
            num_scalar_prefetch=1,
            grid=(CHUNKS * blocks,),
            in_specs=[
                pl.BlockSpec((step // width, rows, width), lambda i, which: (i, 0, 0)),
                pl.BlockSpec((rows, full // 2), lambda i, which: (0, which[0])),
            ],
            out_specs=[pl.BlockSpec((step, full // 2), target(k)) for k in range(CHUNKS)],
        ),
        compiler_params=params(20),
        cost_estimate=cost(rows * full * full, 4 * rows * full + full * full),
    )(which[None].astype(jnp.int32), agg, low)


def outer_halve_kernel(blocks, which, agg_ref, low_ref, *refs):
    i = pl.program_id(0)
    outs = refs[-2 * CHUNKS :]
    for n, out_ref in enumerate(outs):
        came_ref = refs[n // 2]

        @pl.when(i // blocks == n)
        def _():
            total = turned_dot(agg_ref, low_ref) + came_ref[...].astype(F32)
            out_ref[...] = total.astype(out_ref.dtype)


def outer_halve(which, side, agg, low, came, after=()):
    owners, rows, width = agg.shape
    full = owners * width
    step = DEEP
    half = full // CHUNKS // 2
    blocks = half // step

    def row(i, which):
        k = i // (2 * blocks)
        part = i // blocks % 2
        near = jnp.where(k == 0, which[1], which[2])
        return k * 2 * blocks + jnp.where(part == 0, 1 - near, near) * blocks + i % blocks

    def arrived(k):
        def index(i, which):
            inside = clamped(i, k * 2 * blocks, 2 * blocks) + k * 2 * blocks
            return (row(inside, which) - k * 2 * blocks, 0)

        return index

    def target(n):
        return lambda i, which: (clamped(i, n * blocks, blocks), 0)

    outs = pl.pallas_call(
        functools.partial(outer_halve_kernel, blocks),
        name="outer_halve",
        out_shape=[
            jax.ShapeDtypeStruct((half, full // 2), dtype) for dtype in (BF16, F32) * CHUNKS
        ],
        grid_spec=pltpu.PrefetchScalarGridSpec(
            num_scalar_prefetch=1,
            grid=(2 * CHUNKS * blocks,),
            in_specs=[
                pl.BlockSpec(
                    (step // width, rows, width), lambda i, which: (row(i, which), 0, 0)
                ),
                pl.BlockSpec((rows, full // 2), lambda i, which: (0, which[0])),
            ]
            + [pl.BlockSpec((step, full // 2), arrived(k)) for k in range(CHUNKS)]
            + anywhere(after),
            out_specs=[pl.BlockSpec((step, full // 2), target(n)) for n in range(2 * CHUNKS)],
        ),
        compiler_params=params(28),
        cost_estimate=cost(rows * full * full, 4 * rows * full + 4 * full * full),
    )(jnp.stack([which, *side]).astype(jnp.int32), agg, low, *came, *after)
    return outs[0::2], outs[1::2]


def back_kernel(low_ref, w_ref, *refs):
    out_ref = refs[-1]
    parts, _, width = out_ref.shape
    value = dot(low_ref[...], w_ref[...], 1, 1).astype(BF16)
    for k in range(parts):
        out_ref[k] = value[:, k * width : (k + 1) * width]


def back(low, weight, owners, after=()):
    rows, full = low.shape
    width = full // owners
    step = DEEP
    return pl.pallas_call(
        back_kernel,
        name="back",
        out_shape=jax.ShapeDtypeStruct((owners, rows, width), BF16),
        grid=(full // step,),
        in_specs=[
            pl.BlockSpec((rows, full), lambda i: (0, 0)),
            pl.BlockSpec((step, full), lambda i: (i, 0)),
        ]
        + anywhere(after),
        out_specs=pl.BlockSpec((step // width, rows, width), lambda i: (i, 0, 0)),
        compiler_params=params(20),
        cost_estimate=cost(2 * rows * full * full, 2 * full * full + 4 * rows * full),
    )(low, weight, *after)


def split_kernel(value_ref, *refs):
    count = value_ref.shape[1]
    for j, out_ref in enumerate(refs[-count:]):
        out_ref[...] = value_ref[:, j]


def row_step(rows):
    return rows // 2 if rows % 32 == 0 else rows


def split(value, after=()):
    first, second, rows, width = value.shape
    step = row_step(rows)
    return pl.pallas_call(
        split_kernel,
        name="split",
        out_shape=[jax.ShapeDtypeStruct((first, rows, width), BF16)] * second,
        grid=(rows // step,),
        in_specs=[pl.BlockSpec((first, second, step, width), lambda i: (0, 0, i, 0))]
        + anywhere(after),
        out_specs=[pl.BlockSpec((first, step, width), lambda i: (0, i, 0))] * second,
        compiler_params=params(16),
        cost_estimate=cost(0, 4 * value.size),
    )(value, *after)


def swap_with(value, mask):
    count = lax.axis_size("feat")
    return lax.ppermute(value, "feat", [(i, i ^ mask) for i in range(count)])


def scatter(values):
    return [values[0]] + [swap_with(values[k], k) for k in range(1, len(values))]


def outer_exchange(value):
    inner = lax.axis_size("feat") // OUTER
    groups = [[k * inner + low for k in range(OUTER)] for low in range(inner)]
    return lax.all_to_all(
        value, "feat", split_axis=0, concat_axis=0, axis_index_groups=groups, tiled=True
    )


def gather_rows(me, inner, blocks, out_ref):
    for high, low, block in blocks:
        rows = block.shape[0]
        owner = high * inner + (me ^ low)
        out_ref[pl.ds(pl.multiple_of(owner * rows, 16), rows), :] = block[...]


def swap_feat(value, bit):
    return swap_with(value, 1 << bit)


def swap_rep(value):
    return lax.ppermute(value, "rep", [(0, 1), (1, 0)])


def exchange(packed):
    owners = lax.axis_size("feat")
    blocks = packed.reshape(owners, -1, packed.shape[-1])
    return lax.all_to_all(blocks, "feat", split_axis=0, concat_axis=0, tiled=True)


def place_kernel(count, where, *refs):
    out_ref = refs[-1]
    for k in range(count):

        @pl.when(pl.program_id(0) == k)
        def _():
            out_ref[...] = refs[k][...].astype(F32)


def place(where, pieces, before=None, after=()):
    count = len(pieces)
    rows, columns = pieces[0].shape
    step = min(rows, 512)
    steps = rows // step
    full = 2 * columns
    begun = () if before is None else (before,)

    def source(k):
        return lambda i, j, where: (jnp.where(i == k, j, jnp.where(i < k, 0, steps - 1)), 0)

    return pl.pallas_call(
        functools.partial(place_kernel, count),
        name="place",
        out_shape=jax.ShapeDtypeStruct((full, full), F32),
        grid_spec=pltpu.PrefetchScalarGridSpec(
            num_scalar_prefetch=1,
            grid=(count, steps),
            in_specs=[pl.BlockSpec((step, columns), source(k)) for k in range(count)]
            + anywhere(begun)
            + anywhere(after),
            out_specs=pl.BlockSpec(
                (step, columns), lambda i, j, where: (where[i] * steps + j, where[count + i])
            ),
        ),
        input_output_aliases={1 + count: 0} if begun else {},
        compiler_params=params(16),
        cost_estimate=cost(0, 6 * count * rows * columns),
    )(jnp.stack(where).astype(jnp.int32), *pieces, *begun, *after)


def halve_kernel(chunks, side, *refs):
    outs = refs[-2 * chunks :]
    for k in range(chunks):
        for part in range(2):
            kept, came = refs[4 * k + 2 * part], refs[4 * k + 2 * part + 1]
            out = outs[2 * k + part]
            out[...] = (kept[...].astype(F32) + came[...].astype(F32)).astype(out.dtype)


def halve(side, kept, came, after=()):
    chunks = len(kept)
    half, columns = kept[0].shape[0] // 2, kept[0].shape[1]
    step = min(half, 128)
    steps = half // step

    def source(k, part):
        return lambda i, side: ((side[k] if part else 1 - side[k]) * steps + i, 0)

    in_specs = []
    operands = []
    out_shape = []
    for k in range(chunks):
        for part in range(2):
            for value in (kept[k], came[k]):
                in_specs.append(pl.BlockSpec((step, columns), source(k, part)))
                operands.append(value)
        for dtype in (BF16, F32):
            out_shape.append(jax.ShapeDtypeStruct((half, columns), dtype))
    outs = pl.pallas_call(
        functools.partial(halve_kernel, chunks),
        name="halve",
        out_shape=tuple(out_shape),
        grid_spec=pltpu.PrefetchScalarGridSpec(
            num_scalar_prefetch=1,
            grid=(steps,),
            in_specs=in_specs + anywhere(after),
            out_specs=[pl.BlockSpec((step, columns), lambda i, side: (i, 0)) for _ in out_shape],
        ),
        compiler_params=params(16),
        cost_estimate=cost(2 * chunks * half * columns, 18 * chunks * half * columns),
    )(jnp.stack(side).astype(jnp.int32), *operands, *after)
    return outs[0::2], outs[1::2]


def pick_kernel(side, *refs):
    first, second = (refs[2 * k][...] + refs[2 * k + 1][...].astype(F32) for k in range(2))
    away_ref, own_ref = refs[-2:]

    @pl.when(side[0] == 0)
    def _():
        own_ref[...] = first
        away_ref[...] = second.astype(BF16)

    @pl.when(side[0] == 1)
    def _():
        own_ref[...] = second
        away_ref[...] = first.astype(BF16)


def pick(side, kept, came, after=()):
    rows, columns = kept[0].shape
    step = min(rows, 128)
    block = pl.BlockSpec((step, columns), lambda i, side: (i, 0))
    away, own = pl.pallas_call(
        pick_kernel,
        name="pick",
        out_shape=(
            jax.ShapeDtypeStruct((rows, columns), BF16),
            jax.ShapeDtypeStruct((rows, columns), F32),
        ),
        grid_spec=pltpu.PrefetchScalarGridSpec(
            num_scalar_prefetch=1,
            grid=(rows // step,),
            in_specs=[block] * 4 + anywhere(after),
            out_specs=(block, block),
        ),
        compiler_params=params(16),
        cost_estimate=cost(2 * rows * columns, 18 * rows * columns),
    )(side[None].astype(jnp.int32), kept[0], came[0], kept[1], came[1], *after)
    return [away], [own]


def sort_kernel(side, own_ref, other_ref, *refs):
    first_ref, second_ref = refs[-2:]

    @pl.when(side[0] == 0)
    def _():
        first_ref[...] = own_ref[...]
        second_ref[...] = other_ref[...]

    @pl.when(side[0] == 1)
    def _():
        first_ref[...] = other_ref[...]
        second_ref[...] = own_ref[...]


def sort(side, own, other, after=()):
    whole = pl.BlockSpec(own.shape, lambda i, side: (0, 0))
    return pl.pallas_call(
        sort_kernel,
        name="sort",
        out_shape=[jax.ShapeDtypeStruct(own.shape, BF16)] * 2,
        grid_spec=pltpu.PrefetchScalarGridSpec(
            num_scalar_prefetch=1,
            grid=(1,),
            in_specs=[whole, whole] + anywhere(after),
            out_specs=[whole, whole],
        ),
        compiler_params=params(16),
        cost_estimate=cost(0, 8 * own.size),
    )(side[None].astype(jnp.int32), own, other, *after)


def add_kernel(first_ref, second_ref, *refs):
    refs[-1][...] = first_ref[...] + second_ref[...]


def add(first, second, after=()):
    return pl.pallas_call(
        add_kernel,
        name="add",
        out_shape=jax.ShapeDtypeStruct(first.shape, F32),
        in_specs=[pl.BlockSpec(memory_space=pltpu.VMEM)] * 2 + anywhere(after),
        compiler_params=params(16),
        cost_estimate=cost(first.size, 12 * first.size),
    )(first, second, *after)


def close_kernel(chunks, *refs):
    for k in range(chunks):
        total = refs[2 * k][...] + refs[2 * k + 1][...].astype(F32)
        refs[len(refs) - chunks + k][...] = total.astype(BF16)


def close(kept, came, after=()):
    chunks = len(kept)
    pairs = [value for pair in zip(kept, came) for value in pair]
    return pl.pallas_call(
        functools.partial(close_kernel, chunks),
        name="close",
        out_shape=[jax.ShapeDtypeStruct(value.shape, BF16) for value in kept],
        in_specs=[pl.BlockSpec(memory_space=pltpu.VMEM) for _ in pairs] + anywhere(after),
        compiler_params=params(16),
        cost_estimate=cost(kept[0].size * chunks, 8 * kept[0].size * chunks),
    )(*pairs, *after)


def join_kernel(chunks, side, *refs):
    outs = refs[-chunks:]
    for k in range(chunks):
        for part in range(2):

            @pl.when(pl.program_id(0) == part)
            def _():
                outs[k][...] = refs[2 * k + part][...]


def join(side, own, other, after=()):
    chunks = len(own)
    rows, columns = own[0].shape
    step = min(rows, 256)
    steps = rows // step
    pairs = [value for pair in zip(own, other) for value in pair]

    def source(part):
        return lambda i, j, side: (jnp.where(i == part, j, 0 if part else steps - 1), 0)

    def target(k):
        return lambda i, j, side: (jnp.where(i == 0, side[k], 1 - side[k]) * steps + j, 0)

    return pl.pallas_call(
        functools.partial(join_kernel, chunks),
        name="join",
        out_shape=[jax.ShapeDtypeStruct((2 * rows, columns), BF16) for _ in own],
        grid_spec=pltpu.PrefetchScalarGridSpec(
            num_scalar_prefetch=1,
            grid=(2, steps),
            in_specs=[pl.BlockSpec((step, columns), source(n % 2)) for n in range(2 * chunks)]
            + anywhere(after),
            out_specs=[pl.BlockSpec((step, columns), target(k)) for k in range(chunks)],
        ),
        compiler_params=params(16),
        cost_estimate=cost(0, 8 * chunks * rows * columns),
    )(jnp.stack(side).astype(jnp.int32), *pairs, *after)


def run(tiles, features, adjacency, counts, offsets, weight, bias, cotangent):
    owners = lax.axis_size("feat")
    me = lax.axis_index("feat")
    core = lax.axis_index("rep")
    bits = owners.bit_length() - 1
    inner = owners // OUTER
    side = [(me >> bit) & 1 for bit in range(bits)]
    crossed = [1, 0]
    low_bits = (me & (inner - 1)).astype(jnp.int32)
    place_of = low_bits[None]

    cot = pack(tiles, counts, offsets, cotangent)
    agg = exchange(aggregate(tiles, counts, offsets, features, adjacency, cot))
    cot = exchange(cot)
    act, low, grad_bias = middle(place_of, agg, cot, weight, bias)
    sent = outer(1 - core, agg, low)
    came = [swap_rep(value) for value in sent]
    act, _ = lax.optimization_barrier((act, sent[0]))
    act = outer_exchange(act)

    came_bias = swap_rep(grad_bias)
    away, kept = outer_halve(core, side[:2], agg, low, came)
    came = [swap_feat(away[k], k) for k in range(2)]
    back_rows = back(low, weight, owners, away)
    grad_bias = add(grad_bias, came_bias, (back_rows,))
    came_bias = swap_feat(grad_bias, 0)
    away, kept = halve([side[1], side[0]], kept, came, (grad_bias,))
    came = [swap_feat(away[k], crossed[k]) for k in range(2)]
    grad_bias = add(grad_bias, came_bias, away)
    came_bias = swap_feat(grad_bias, 1)
    away, kept = pick(side[2], kept, came, (grad_bias,))
    came = [swap_feat(away[0], 2)]
    act = split(act, away)
    grad_bias = add(grad_bias, came_bias, (act[0],))
    act = scatter(act)
    for bit in range(3, bits):
        came_bias = swap_feat(grad_bias, bit - 1)
        away, kept = halve(side[bit : bit + 1], kept, came, (grad_bias,))
        came = [swap_feat(away[0], bit)]
        grad_bias = add(grad_bias, came_bias, away)
    came_bias = swap_feat(grad_bias, bits - 1)
    grad_bias = add(grad_bias, came_bias, away)
    owned = close(kept, came, (grad_bias,))
    for bit in reversed(range(3, bits)):
        owned = join(side[bit : bit + 1], owned, [swap_feat(owned[0], bit)])
    other = swap_feat(owned[0], 2)
    activations = unpack(features.shape, counts, offsets, place_of, act, owned)
    owned = sort(side[2], owned[0], other, (activations,))
    other = [swap_feat(owned[k], crossed[k]) for k in range(2)]
    back_rows, owned = lax.optimization_barrier((back_rows, owned))
    back_rows = exchange(back_rows).reshape(tiles * TILE, -1)
    owned = join([side[1], side[0]], owned, other)
    across = [swap_rep(value) for value in owned]
    far = [swap_feat(owned[k], k) for k in range(2)]
    near_rows = [2 * k + side[k] for k in range(2)]
    far_rows = [2 * k + 1 - side[k] for k in range(2)]
    columns = [core] * 2 + [1 - core] * 2
    grad_weight = place(2 * near_rows + columns, [*owned, *across])
    grad_features = spread(counts, offsets, back_rows, adjacency, (grad_weight,))
    far, grad_features = lax.optimization_barrier((far, grad_features))
    far_across = [swap_rep(value) for value in far]
    grad_weight = place(2 * far_rows + columns, [*far, *far_across], grad_weight)
    return activations, grad_features, grad_weight, grad_bias[0]


def local(features, adjacency, counts, weight, bias, cotangent):
    features = features.transpose(1, 0, 2)
    cotangent = cotangent.transpose(1, 0, 2)
    clusters, _, nodes = features.shape
    used = (counts + TILE - 1) // TILE
    before = jnp.arange(clusters)[None] < jnp.arange(clusters + 1)[:, None]
    offsets = jnp.sum(jnp.where(before, used[None], 0), axis=1).astype(jnp.int32)
    need = offsets[-1:]
    need = jnp.maximum(need, swap_rep(need))[0]
    most = clusters * nodes // TILE
    unit = max(2, 16 * lax.axis_size("feat") // TILE)
    buckets = [b for b in BUCKETS if b < most and b % unit == 0] + [most]
    ordered = sorted(buckets)
    branch = jnp.int32(buckets.index(ordered[0]))
    for low, high in zip(ordered, ordered[1:]):
        branch = jnp.where(need > low, buckets.index(high), branch)
    branches = [functools.partial(run, b) for b in buckets]
    args = (features, adjacency, counts, offsets, weight, bias, cotangent)
    activations, grad_features, grad_weight, grad_bias = lax.switch(branch, branches, *args)
    return (
        activations.transpose(1, 0, 2),
        grad_features.transpose(1, 0, 2),
        grad_weight,
        grad_bias,
    )


def solution(mesh):
    placed = (
        P("feat", "rep", None),
        P("rep", None, None),
        P("rep"),
        P(),
        P(),
        P("feat", "rep", None),
    )
    return jax.shard_map(
        local,
        mesh=mesh,
        in_specs=placed,
        out_specs=(P("feat", "rep", None), P("feat", "rep", None), P(), P()),
        check_vma=False,
    )
```

```python
import functools

import jax
import jax.numpy as jnp
from jax import lax
from jax.experimental import pallas as pl
from jax.experimental.pallas import tpu as pltpu
from jax.sharding import PartitionSpec as P

TILE = 128
ROWS = 512
SIDE = 512
OUTER = 4
SLAB = 128
DEEP = 512
CHUNKS = 2
F32 = jnp.float32
BF16 = jnp.bfloat16
BUCKETS = (64,)


def params(mib=60):
    return pltpu.CompilerParams(vmem_limit_bytes=mib * 1024 * 1024)


def cost(flops, moved, transcendentals=0):
    return pl.CostEstimate(flops=flops, bytes_accessed=moved, transcendentals=transcendentals)


def dot(a, b, ca, cb):
    return lax.dot_general(a, b, (((ca,), (cb,)), ((), ())), preferred_element_type=F32)


def anywhere(values):
    return [pl.BlockSpec(memory_space=pl.ANY) for _ in values]


def eye():
    row = lax.broadcasted_iota(jnp.int32, (TILE, TILE), 0)
    return row == lax.broadcasted_iota(jnp.int32, (TILE, TILE), 1)


def aligned(index, size=TILE):
    return pl.ds(pl.multiple_of(index * TILE, TILE), size)


def by_groups(first, last, one, size=4):
    groups = (last - first) // size

    def group(n, carry):
        for k in range(size):
            one(first + n * size + k)
        return carry

    def single(t, carry):
        one(t)
        return carry

    lax.fori_loop(0, groups, group, 0)
    lax.fori_loop(first + groups * size, last, single, 0)


def clear_tail(out_ref, first, last):
    def one(p):
        out_ref[aligned(p), :] = jnp.zeros((TILE, out_ref.shape[1]), out_ref.dtype)

    by_groups(first, last, one)


def pack_kernel(clusters, counts, offsets, in_ref, out_ref):
    features = in_ref.shape[1]
    for c in range(clusters):
        live = counts[c]
        start = offsets[c]

        def one(t):
            lane = t * TILE + lax.broadcasted_iota(jnp.int32, (features, TILE), 1)
            block = jnp.where(lane < live, in_ref[c, :, aligned(t)].astype(F32), 0.0)
            out_ref[aligned(start + t), :] = block.T.astype(out_ref.dtype)

        by_groups(0, offsets[c + 1] - start, one)
    clear_tail(out_ref, offsets[clusters], out_ref.shape[0] // TILE)


def pack(tiles, counts, offsets, values):
    clusters, features, nodes = values.shape
    size = tiles * TILE * features
    return pl.pallas_call(
        functools.partial(pack_kernel, clusters),
        name="pack",
        out_shape=jax.ShapeDtypeStruct((tiles * TILE, features), BF16),
        grid_spec=pltpu.PrefetchScalarGridSpec(
            num_scalar_prefetch=2,
            grid=(1,),
            in_specs=[pl.BlockSpec((clusters, features, nodes), lambda i, *_: (0, 0, 0))],
            out_specs=pl.BlockSpec((tiles * TILE, features), lambda i, *_: (0, 0)),
        ),
        compiler_params=params(16),
        cost_estimate=cost(size, 4 * size),
    )(counts, offsets, values)


def unpack_kernel(count, counts, offsets, me, *refs):
    out_ref, packed = refs[-2:]
    c = pl.program_id(0)
    features = out_ref.shape[1]
    live = counts[c]
    start = offsets[c]

    @pl.when(c == 0)
    def _():
        blocks = [(k, low, refs[low].at[k]) for low in range(count) for k in range(OUTER)]
        gather_rows(me[0], count, blocks, packed)

    def one(t):
        lane = t * TILE + lax.broadcasted_iota(jnp.int32, (features, TILE), 1)
        block = packed[aligned(start + t), :].astype(F32).T
        out_ref[0, :, aligned(t)] = jnp.where(lane < live, block, 0.0)

    def clear(t):
        out_ref[0, :, aligned(t)] = jnp.zeros((features, TILE), F32)

    used = offsets[c + 1] - start
    by_groups(0, used, one)
    by_groups(used, out_ref.shape[2] // TILE, clear)


def unpack(shape, counts, offsets, me, values, after=()):
    clusters, features, nodes = shape
    count = len(values)
    size = count * values[0].size
    whole = pl.BlockSpec(values[0].shape, lambda c, *_: (0, 0, 0))
    return pl.pallas_call(
        functools.partial(unpack_kernel, count),
        name="unpack",
        out_shape=jax.ShapeDtypeStruct(shape, F32),
        grid_spec=pltpu.PrefetchScalarGridSpec(
            num_scalar_prefetch=3,
            grid=(clusters,),
            in_specs=[whole] * count + anywhere(after),
            out_specs=pl.BlockSpec((1, features, nodes), lambda c, *_: (c, 0, 0)),
            scratch_shapes=[pltpu.VMEM((size // features, features), BF16)],
        ),
        compiler_params=params(16),
        cost_estimate=cost(size, 2 * size + 4 * clusters * features * nodes),
    )(counts, offsets, me, *values, *after)


def adjacency_spec(nodes):
    def index(c, i, counts, offsets):
        return (c, jnp.minimum(i, (counts[c] - 1) // ROWS), 0)

    return pl.BlockSpec((1, ROWS, nodes), index)


def aggregate_kernel(clusters, counts, offsets, x_ref, a_ref, *refs):
    out_ref, masked = refs[-2:]
    c = pl.program_id(0)
    i = pl.program_id(1)
    live = counts[c]

    @pl.when(jnp.logical_and(c == 0, i == 0))
    def _():
        clear_tail(out_ref, offsets[clusters], out_ref.shape[0] // TILE)

    @pl.when(i == 0)
    def _():
        lane = lax.broadcasted_iota(jnp.int32, masked.shape, 1)
        masked[...] = jnp.where(lane < live, x_ref[0].astype(F32), 0.0).astype(BF16)

    @pl.when(i * ROWS < live)
    def _():
        total = dot(a_ref[0], masked[...], 1, 1)
        for s in range(ROWS // TILE):
            t = i * (ROWS // TILE) + s

            @pl.when(t * TILE < live)
            def _():
                block = a_ref[0, s * TILE : (s + 1) * TILE, aligned(t)]
                block = jnp.where(eye(), block.astype(F32), 0.0).astype(BF16)
                extra = dot(block, masked[:, aligned(t)], 1, 1)
                rows = total[s * TILE : (s + 1) * TILE] + extra
                out_ref[aligned(offsets[c] + t), :] = rows.astype(BF16)


def aggregate(tiles, counts, offsets, features, adjacency, after):
    clusters, width, nodes = features.shape
    return pl.pallas_call(
        functools.partial(aggregate_kernel, clusters),
        name="aggregate",
        out_shape=jax.ShapeDtypeStruct((tiles * TILE, width), BF16),
        grid_spec=pltpu.PrefetchScalarGridSpec(
            num_scalar_prefetch=2,
            grid=(clusters, nodes // ROWS),
            in_specs=[
                pl.BlockSpec((1, width, nodes), lambda c, i, *_: (c, 0, 0)),
                adjacency_spec(nodes),
                *anywhere((after,)),
            ],
            out_specs=pl.BlockSpec((tiles * TILE, width), lambda c, i, *_: (0, 0)),
            scratch_shapes=[pltpu.VMEM((width, nodes), BF16)],
        ),
        compiler_params=params(16),
        cost_estimate=cost(2 * adjacency.size * width, 2 * adjacency.size),
    )(counts, offsets, features, adjacency, after)


def spread_kernel(clusters, counts, offsets, packed, a_ref, *refs):
    out_ref, turned, held, sems = refs[-4:]
    c = pl.program_id(0)
    slot = lax.rem(c, 2)
    live = counts[c]
    width, nodes = turned.shape
    sizes = range(SIDE, nodes + SIDE, SIDE)

    def each(cluster, act):
        need = counts[cluster]
        for size in sizes:

            @pl.when(jnp.logical_and(need > size - SIDE, need <= size))
            def _():
                act(size)

    def copy(cluster, place, size):
        area = (slice(0, size), slice(0, size))
        return pltpu.make_async_copy(
            a_ref.at[(cluster, *area)], held.at[(place, *area)], sems.at[place]
        )

    @pl.when(c == 0)
    def _():
        each(c, lambda size: copy(c, slot, size).start())

    @pl.when(c + 1 < clusters)
    def _():
        each(c + 1, lambda size: copy(c + 1, 1 - slot, size).start())

    start = offsets[c]
    used = offsets[c + 1] - start

    def turn(t):
        lane = t * TILE + lax.broadcasted_iota(jnp.int32, (width, TILE), 1)
        block = packed[aligned(start + t), :].astype(F32).T
        turned[:, aligned(t)] = jnp.where(lane < live, block, 0.0).astype(BF16)

    def clear(t):
        turned[:, aligned(t)] = jnp.zeros((width, TILE), BF16)

    by_groups(0, used, turn)
    by_groups(used, nodes // TILE, clear)

    def compute(size):
        copy(c, slot, size).wait()
        for j in range(0, size, SIDE):
            total = dot(turned[:, :size], held[slot, :size, j : j + SIDE], 1, 0)
            for t in range(j, j + SIDE, TILE):
                block = held[slot, t : t + TILE, t : t + TILE].astype(F32)
                diagonal = jnp.sum(jnp.where(eye(), block, 0.0), axis=0, keepdims=True)
                extra = diagonal * turned[:, t : t + TILE].astype(F32)
                lane = t + lax.broadcasted_iota(jnp.int32, (width, TILE), 1)
                value = total[:, t - j : t - j + TILE] + extra
                out_ref[0, :, t : t + TILE] = jnp.where(lane < live, value, 0.0)
        if size < nodes:
            out_ref[0, :, size:] = jnp.zeros((width, nodes - size), F32)

    each(c, compute)


def spread(counts, offsets, packed, adjacency, after=()):
    clusters, nodes, _ = adjacency.shape
    width = packed.shape[1]
    return pl.pallas_call(
        functools.partial(spread_kernel, clusters),
        name="spread",
        out_shape=jax.ShapeDtypeStruct((clusters, width, nodes), F32),
        grid_spec=pltpu.PrefetchScalarGridSpec(
            num_scalar_prefetch=2,
            grid=(clusters,),
            in_specs=[pl.BlockSpec(packed.shape, lambda c, *_: (0, 0))]
            + anywhere((adjacency, *after)),
            out_specs=pl.BlockSpec((1, width, nodes), lambda c, *_: (c, 0, 0)),
            scratch_shapes=[
                pltpu.VMEM((width, nodes), BF16),
                pltpu.VMEM((2, nodes, nodes), BF16),
                pltpu.SemaphoreType.DMA((2,)),
            ],
        ),
        compiler_params=params(32),
        cost_estimate=cost(2 * adjacency.size * width, 2 * adjacency.size),
    )(counts, offsets, packed, adjacency, *after)


def normal(value):
    bell = jnp.exp(-0.5 * value * value)
    t = 1.0 / (1.0 + (0.3275911 * 0.5**0.5) * jnp.abs(value))
    tail = 0.5 * 1.061405429
    for term in (-1.453152027, 1.421413741, -0.284496736, 0.254829592):
        tail = tail * t + 0.5 * term
    tail = tail * t * bell
    return jnp.where(value >= 0.0, 1.0 - tail, tail), bell * 0.3989422804014327


def middle_kernel(me, agg_ref, cot_ref, w_ref, b_ref, act_ref, low_ref, bias_ref, held, product):
    owners, rows, width = agg_ref.shape

    @pl.when(pl.program_id(0) == 0)
    def _():
        for s in range(owners):
            held[:, s * width : (s + 1) * width] = agg_ref[s]

    parts = cot_ref.shape[0]
    total = jnp.zeros((1, w_ref.shape[1]), F32)
    product[...] = dot(held[...], w_ref[...], 1, 0)
    step = SLAB
    for r in range(0, rows, step):
        pre = product[r : r + step] + b_ref[...].astype(F32)
        cdf, pdf = normal(pre)
        act = (pre * cdf).astype(BF16)
        cot = jnp.concatenate([cot_ref[k, r : r + step] for k in range(parts)], axis=1).astype(F32)
        grad = cot * (cdf + pre * pdf)
        for k in range(parts):
            act_ref[0, k ^ me[0], r : r + step] = act[:, k * width : (k + 1) * width]
        low_ref[r : r + step] = grad.astype(BF16)
        total = total + jnp.sum(grad, axis=0, keepdims=True)
    bias_ref[...] = total


def middle(me, agg, cot, weight, bias):
    owners, rows, width = agg.shape
    full = owners * width
    inner = owners // OUTER
    block = inner * width
    return pl.pallas_call(
        middle_kernel,
        name="middle",
        out_shape=(
            jax.ShapeDtypeStruct((OUTER, inner, rows, width), BF16),
            jax.ShapeDtypeStruct((rows, full), BF16),
            jax.ShapeDtypeStruct((1, full), F32),
        ),
        grid_spec=pltpu.PrefetchScalarGridSpec(
            num_scalar_prefetch=1,
            grid=(OUTER,),
            in_specs=[
                pl.BlockSpec((owners, rows, width), lambda g, me: (0, 0, 0)),
                pl.BlockSpec((inner, rows, width), lambda g, me: (g, 0, 0)),
                pl.BlockSpec((full, block), lambda g, me: (0, g)),
                pl.BlockSpec((1, block), lambda g, me: (0, g)),
            ],
            out_specs=(
                pl.BlockSpec((1, inner, rows, width), lambda g, me: (g, 0, 0, 0)),
                pl.BlockSpec((rows, block), lambda g, me: (0, g)),
                pl.BlockSpec((1, block), lambda g, me: (0, g)),
            ),
            scratch_shapes=[pltpu.VMEM((rows, full), BF16), pltpu.VMEM((rows, block), F32)],
        ),
        compiler_params=params(28),
        cost_estimate=cost(2 * rows * full * full, 2 * full * full + 8 * rows * full),
    )(me, agg, cot, weight, bias[None])


def turned_dot(agg_ref, low_ref):
    left = jnp.concatenate([agg_ref[s].T for s in range(agg_ref.shape[0])], axis=0)
    return dot(left, low_ref[...], 1, 0)


def clamped(i, first, count):
    return jnp.clip(i - first, 0, count - 1)


def outer_kernel(blocks, which, agg_ref, low_ref, *out_refs):
    for k, out_ref in enumerate(out_refs):

        @pl.when(pl.program_id(0) // blocks == k)
        def _():
            out_ref[...] = turned_dot(agg_ref, low_ref).astype(BF16)


def outer(which, agg, low):
    owners, rows, width = agg.shape
    full = owners * width
    step = DEEP
    share = full // CHUNKS
    blocks = share // step

    def target(k):
        return lambda i, which: (clamped(i, k * blocks, blocks), 0)

    return pl.pallas_call(
        functools.partial(outer_kernel, blocks),
        name="outer",
        out_shape=[jax.ShapeDtypeStruct((share, full // 2), BF16)] * CHUNKS,
        grid_spec=pltpu.PrefetchScalarGridSpec(
            num_scalar_prefetch=1,
            grid=(CHUNKS * blocks,),
            in_specs=[
                pl.BlockSpec((step // width, rows, width), lambda i, which: (i, 0, 0)),
                pl.BlockSpec((rows, full // 2), lambda i, which: (0, which[0])),
            ],
            out_specs=[pl.BlockSpec((step, full // 2), target(k)) for k in range(CHUNKS)],
        ),
        compiler_params=params(20),
        cost_estimate=cost(rows * full * full, 4 * rows * full + full * full),
    )(which[None].astype(jnp.int32), agg, low)


def outer_halve_kernel(blocks, which, agg_ref, low_ref, *refs):
    i = pl.program_id(0)
    outs = refs[-2 * CHUNKS :]
    for n, out_ref in enumerate(outs):
        came_ref = refs[n // 2]

        @pl.when(i // blocks == n)
        def _():
            total = turned_dot(agg_ref, low_ref) + came_ref[...].astype(F32)
            out_ref[...] = total.astype(out_ref.dtype)


def outer_halve(which, side, agg, low, came, after=()):
    owners, rows, width = agg.shape
    full = owners * width
    step = DEEP
    half = full // CHUNKS // 2
    blocks = half // step

    def row(i, which):
        k = i // (2 * blocks)
        part = i // blocks % 2
        near = jnp.where(k == 0, which[1], which[2])
        return k * 2 * blocks + jnp.where(part == 0, 1 - near, near) * blocks + i % blocks

    def arrived(k):
        def index(i, which):
            inside = clamped(i, k * 2 * blocks, 2 * blocks) + k * 2 * blocks
            return (row(inside, which) - k * 2 * blocks, 0)

        return index

    def target(n):
        return lambda i, which: (clamped(i, n * blocks, blocks), 0)

    outs = pl.pallas_call(
        functools.partial(outer_halve_kernel, blocks),
        name="outer_halve",
        out_shape=[
            jax.ShapeDtypeStruct((half, full // 2), dtype) for dtype in (BF16, F32) * CHUNKS
        ],
        grid_spec=pltpu.PrefetchScalarGridSpec(
            num_scalar_prefetch=1,
            grid=(2 * CHUNKS * blocks,),
            in_specs=[
                pl.BlockSpec(
                    (step // width, rows, width), lambda i, which: (row(i, which), 0, 0)
                ),
                pl.BlockSpec((rows, full // 2), lambda i, which: (0, which[0])),
            ]
            + [pl.BlockSpec((step, full // 2), arrived(k)) for k in range(CHUNKS)]
            + anywhere(after),
            out_specs=[pl.BlockSpec((step, full // 2), target(n)) for n in range(2 * CHUNKS)],
        ),
        compiler_params=params(28),
        cost_estimate=cost(rows * full * full, 4 * rows * full + 4 * full * full),
    )(jnp.stack([which, *side]).astype(jnp.int32), agg, low, *came, *after)
    return outs[0::2], outs[1::2]


def back_kernel(low_ref, w_ref, *refs):
    out_ref = refs[-1]
    parts, _, width = out_ref.shape
    value = dot(low_ref[...], w_ref[...], 1, 1).astype(BF16)
    for k in range(parts):
        out_ref[k] = value[:, k * width : (k + 1) * width]


def back(low, weight, owners, after=()):
    rows, full = low.shape
    width = full // owners
    step = DEEP
    return pl.pallas_call(
        back_kernel,
        name="back",
        out_shape=jax.ShapeDtypeStruct((owners, rows, width), BF16),
        grid=(full // step,),
        in_specs=[
            pl.BlockSpec((rows, full), lambda i: (0, 0)),
            pl.BlockSpec((step, full), lambda i: (i, 0)),
        ]
        + anywhere(after),
        out_specs=pl.BlockSpec((step // width, rows, width), lambda i: (i, 0, 0)),
        compiler_params=params(20),
        cost_estimate=cost(2 * rows * full * full, 2 * full * full + 4 * rows * full),
    )(low, weight, *after)


def split_kernel(value_ref, *refs):
    count = value_ref.shape[1]
    for j, out_ref in enumerate(refs[-count:]):
        out_ref[...] = value_ref[:, j]


def row_step(rows):
    return rows // 2 if rows % 32 == 0 else rows


def split(value, after=()):
    first, second, rows, width = value.shape
    step = row_step(rows)
    return pl.pallas_call(
        split_kernel,
        name="split",
        out_shape=[jax.ShapeDtypeStruct((first, rows, width), BF16)] * second,
        grid=(rows // step,),
        in_specs=[pl.BlockSpec((first, second, step, width), lambda i: (0, 0, i, 0))]
        + anywhere(after),
        out_specs=[pl.BlockSpec((first, step, width), lambda i: (0, i, 0))] * second,
        compiler_params=params(16),
        cost_estimate=cost(0, 4 * value.size),
    )(value, *after)


def swap_with(value, mask):
    count = lax.axis_size("feat")
    return lax.ppermute(value, "feat", [(i, i ^ mask) for i in range(count)])


def scatter(values):
    return [values[0]] + [swap_with(values[k], k) for k in range(1, len(values))]


def outer_exchange(value):
    inner = lax.axis_size("feat") // OUTER
    groups = [[k * inner + low for k in range(OUTER)] for low in range(inner)]
    return lax.all_to_all(
        value, "feat", split_axis=0, concat_axis=0, axis_index_groups=groups, tiled=True
    )


def gather_rows(me, inner, blocks, out_ref):
    for high, low, block in blocks:
        rows = block.shape[0]
        owner = high * inner + (me ^ low)
        out_ref[pl.ds(pl.multiple_of(owner * rows, 16), rows), :] = block[...]


def swap_feat(value, bit):
    return swap_with(value, 1 << bit)


def swap_rep(value):
    return lax.ppermute(value, "rep", [(0, 1), (1, 0)])


def exchange(packed):
    owners = lax.axis_size("feat")
    blocks = packed.reshape(owners, -1, packed.shape[-1])
    return lax.all_to_all(blocks, "feat", split_axis=0, concat_axis=0, tiled=True)


def place_kernel(count, where, *refs):
    out_ref = refs[-1]
    for k in range(count):

        @pl.when(pl.program_id(0) == k)
        def _():
            out_ref[...] = refs[k][...].astype(F32)


def place(where, pieces, before=None, after=()):
    count = len(pieces)
    rows, columns = pieces[0].shape
    step = min(rows, 512)
    steps = rows // step
    full = 2 * columns
    begun = () if before is None else (before,)

    def source(k):
        return lambda i, j, where: (jnp.where(i == k, j, jnp.where(i < k, 0, steps - 1)), 0)

    return pl.pallas_call(
        functools.partial(place_kernel, count),
        name="place",
        out_shape=jax.ShapeDtypeStruct((full, full), F32),
        grid_spec=pltpu.PrefetchScalarGridSpec(
            num_scalar_prefetch=1,
            grid=(count, steps),
            in_specs=[pl.BlockSpec((step, columns), source(k)) for k in range(count)]
            + anywhere(begun)
            + anywhere(after),
            out_specs=pl.BlockSpec(
                (step, columns), lambda i, j, where: (where[i] * steps + j, where[count + i])
            ),
        ),
        input_output_aliases={1 + count: 0} if begun else {},
        compiler_params=params(16),
        cost_estimate=cost(0, 6 * count * rows * columns),
    )(jnp.stack(where).astype(jnp.int32), *pieces, *begun, *after)


def halve_kernel(chunks, side, *refs):
    outs = refs[-2 * chunks :]
    for k in range(chunks):
        for part in range(2):
            kept, came = refs[4 * k + 2 * part], refs[4 * k + 2 * part + 1]
            out = outs[2 * k + part]
            out[...] = (kept[...].astype(F32) + came[...].astype(F32)).astype(out.dtype)


def halve(side, kept, came, after=()):
    chunks = len(kept)
    half, columns = kept[0].shape[0] // 2, kept[0].shape[1]
    step = min(half, 128)
    steps = half // step

    def source(k, part):
        return lambda i, side: ((side[k] if part else 1 - side[k]) * steps + i, 0)

    in_specs = []
    operands = []
    out_shape = []
    for k in range(chunks):
        for part in range(2):
            for value in (kept[k], came[k]):
                in_specs.append(pl.BlockSpec((step, columns), source(k, part)))
                operands.append(value)
        for dtype in (BF16, F32):
            out_shape.append(jax.ShapeDtypeStruct((half, columns), dtype))
    outs = pl.pallas_call(
        functools.partial(halve_kernel, chunks),
        name="halve",
        out_shape=tuple(out_shape),
        grid_spec=pltpu.PrefetchScalarGridSpec(
            num_scalar_prefetch=1,
            grid=(steps,),
            in_specs=in_specs + anywhere(after),
            out_specs=[pl.BlockSpec((step, columns), lambda i, side: (i, 0)) for _ in out_shape],
        ),
        compiler_params=params(16),
        cost_estimate=cost(2 * chunks * half * columns, 18 * chunks * half * columns),
    )(jnp.stack(side).astype(jnp.int32), *operands, *after)
    return outs[0::2], outs[1::2]


def pick_kernel(side, *refs):
    first, second = (refs[2 * k][...] + refs[2 * k + 1][...].astype(F32) for k in range(2))
    away_ref, own_ref = refs[-2:]

    @pl.when(side[0] == 0)
    def _():
        own_ref[...] = first
        away_ref[...] = second.astype(BF16)

    @pl.when(side[0] == 1)
    def _():
        own_ref[...] = second
        away_ref[...] = first.astype(BF16)


def pick(side, kept, came, after=()):
    rows, columns = kept[0].shape
    step = min(rows, 128)
    block = pl.BlockSpec((step, columns), lambda i, side: (i, 0))
    away, own = pl.pallas_call(
        pick_kernel,
        name="pick",
        out_shape=(
            jax.ShapeDtypeStruct((rows, columns), BF16),
            jax.ShapeDtypeStruct((rows, columns), F32),
        ),
        grid_spec=pltpu.PrefetchScalarGridSpec(
            num_scalar_prefetch=1,
            grid=(rows // step,),
            in_specs=[block] * 4 + anywhere(after),
            out_specs=(block, block),
        ),
        compiler_params=params(16),
        cost_estimate=cost(2 * rows * columns, 18 * rows * columns),
    )(side[None].astype(jnp.int32), kept[0], came[0], kept[1], came[1], *after)
    return [away], [own]


def sort_kernel(side, own_ref, other_ref, *refs):
    first_ref, second_ref = refs[-2:]

    @pl.when(side[0] == 0)
    def _():
        first_ref[...] = own_ref[...]
        second_ref[...] = other_ref[...]

    @pl.when(side[0] == 1)
    def _():
        first_ref[...] = other_ref[...]
        second_ref[...] = own_ref[...]


def sort(side, own, other, after=()):
    whole = pl.BlockSpec(own.shape, lambda i, side: (0, 0))
    return pl.pallas_call(
        sort_kernel,
        name="sort",
        out_shape=[jax.ShapeDtypeStruct(own.shape, BF16)] * 2,
        grid_spec=pltpu.PrefetchScalarGridSpec(
            num_scalar_prefetch=1,
            grid=(1,),
            in_specs=[whole, whole] + anywhere(after),
            out_specs=[whole, whole],
        ),
        compiler_params=params(16),
        cost_estimate=cost(0, 8 * own.size),
    )(side[None].astype(jnp.int32), own, other, *after)


def add_kernel(first_ref, second_ref, *refs):
    refs[-1][...] = first_ref[...] + second_ref[...]


def add(first, second, after=()):
    return pl.pallas_call(
        add_kernel,
        name="add",
        out_shape=jax.ShapeDtypeStruct(first.shape, F32),
        in_specs=[pl.BlockSpec(memory_space=pltpu.VMEM)] * 2 + anywhere(after),
        compiler_params=params(16),
        cost_estimate=cost(first.size, 12 * first.size),
    )(first, second, *after)


def close_kernel(chunks, *refs):
    for k in range(chunks):
        total = refs[2 * k][...] + refs[2 * k + 1][...].astype(F32)
        refs[len(refs) - chunks + k][...] = total.astype(BF16)


def close(kept, came, after=()):
    chunks = len(kept)
    pairs = [value for pair in zip(kept, came) for value in pair]
    return pl.pallas_call(
        functools.partial(close_kernel, chunks),
        name="close",
        out_shape=[jax.ShapeDtypeStruct(value.shape, BF16) for value in kept],
        in_specs=[pl.BlockSpec(memory_space=pltpu.VMEM) for _ in pairs] + anywhere(after),
        compiler_params=params(16),
        cost_estimate=cost(kept[0].size * chunks, 8 * kept[0].size * chunks),
    )(*pairs, *after)


def join_kernel(chunks, side, *refs):
    outs = refs[-chunks:]
    for k in range(chunks):
        for part in range(2):

            @pl.when(pl.program_id(0) == part)
            def _():
                outs[k][...] = refs[2 * k + part][...]


def join(side, own, other, after=()):
    chunks = len(own)
    rows, columns = own[0].shape
    step = min(rows, 256)
    steps = rows // step
    pairs = [value for pair in zip(own, other) for value in pair]

    def source(part):
        return lambda i, j, side: (jnp.where(i == part, j, 0 if part else steps - 1), 0)

    def target(k):
        return lambda i, j, side: (jnp.where(i == 0, side[k], 1 - side[k]) * steps + j, 0)

    return pl.pallas_call(
        functools.partial(join_kernel, chunks),
        name="join",
        out_shape=[jax.ShapeDtypeStruct((2 * rows, columns), BF16) for _ in own],
        grid_spec=pltpu.PrefetchScalarGridSpec(
            num_scalar_prefetch=1,
            grid=(2, steps),
            in_specs=[pl.BlockSpec((step, columns), source(n % 2)) for n in range(2 * chunks)]
            + anywhere(after),
            out_specs=[pl.BlockSpec((step, columns), target(k)) for k in range(chunks)],
        ),
        compiler_params=params(16),
        cost_estimate=cost(0, 8 * chunks * rows * columns),
    )(jnp.stack(side).astype(jnp.int32), *pairs, *after)


def run(tiles, features, adjacency, counts, offsets, weight, bias, cotangent):
    owners = lax.axis_size("feat")
    me = lax.axis_index("feat")
    core = lax.axis_index("rep")
    bits = owners.bit_length() - 1
    inner = owners // OUTER
    side = [(me >> bit) & 1 for bit in range(bits)]
    crossed = [1, 0]
    low_bits = (me & (inner - 1)).astype(jnp.int32)
    place_of = low_bits[None]

    cot = pack(tiles, counts, offsets, cotangent)
    agg = exchange(aggregate(tiles, counts, offsets, features, adjacency, cot))
    cot = exchange(cot)
    act, low, grad_bias = middle(place_of, agg, cot, weight, bias)
    sent = outer(1 - core, agg, low)
    came = [swap_rep(value) for value in sent]
    act, _ = lax.optimization_barrier((act, sent[0]))
    act = outer_exchange(act)

    came_bias = swap_rep(grad_bias)
    away, kept = outer_halve(core, side[:2], agg, low, came)
    came = [swap_feat(away[k], k) for k in range(2)]
    back_rows = back(low, weight, owners, away)
    grad_bias = add(grad_bias, came_bias, (back_rows,))
    came_bias = swap_feat(grad_bias, 0)
    away, kept = halve([side[1], side[0]], kept, came, (grad_bias,))
    came = [swap_feat(away[k], crossed[k]) for k in range(2)]
    grad_bias = add(grad_bias, came_bias, away)
    came_bias = swap_feat(grad_bias, 1)
    away, kept = pick(side[2], kept, came, (grad_bias,))
    came = [swap_feat(away[0], 2)]
    act = split(act, away)
    grad_bias = add(grad_bias, came_bias, (act[0],))
    act = scatter(act)
    for bit in range(3, bits):
        came_bias = swap_feat(grad_bias, bit - 1)
        away, kept = halve(side[bit : bit + 1], kept, came, (grad_bias,))
        came = [swap_feat(away[0], bit)]
        grad_bias = add(grad_bias, came_bias, away)
    came_bias = swap_feat(grad_bias, bits - 1)
    grad_bias = add(grad_bias, came_bias, away)
    owned = close(kept, came, (grad_bias,))
    for bit in reversed(range(3, bits)):
        owned = join(side[bit : bit + 1], owned, [swap_feat(owned[0], bit)])
    other = swap_feat(owned[0], 2)
    activations = unpack(features.shape, counts, offsets, place_of, act, owned)
    owned = sort(side[2], owned[0], other, (activations,))
    other = [swap_feat(owned[k], crossed[k]) for k in range(2)]
    back_rows, owned = lax.optimization_barrier((back_rows, owned))
    back_rows = exchange(back_rows).reshape(tiles * TILE, -1)
    owned = join([side[1], side[0]], owned, other)
    across = [swap_rep(value) for value in owned]
    far = [swap_feat(owned[k], k) for k in range(2)]
    near_rows = [2 * k + side[k] for k in range(2)]
    far_rows = [2 * k + 1 - side[k] for k in range(2)]
    columns = [core] * 2 + [1 - core] * 2
    grad_weight = place(2 * near_rows + columns, [*owned, *across])
    grad_features = spread(counts, offsets, back_rows, adjacency, (grad_weight,))
    far, grad_features = lax.optimization_barrier((far, grad_features))
    far_across = [swap_rep(value) for value in far]
    grad_weight = place(2 * far_rows + columns, [*far, *far_across], grad_weight)
    return activations, grad_features, grad_weight, grad_bias[0]


def local(features, adjacency, counts, weight, bias, cotangent):
    features = features.transpose(1, 0, 2)
    cotangent = cotangent.transpose(1, 0, 2)
    clusters, _, nodes = features.shape
    used = (counts + TILE - 1) // TILE
    before = jnp.arange(clusters)[None] < jnp.arange(clusters + 1)[:, None]
    offsets = jnp.sum(jnp.where(before, used[None], 0), axis=1).astype(jnp.int32)
    need = offsets[-1:]
    need = jnp.maximum(need, swap_rep(need))[0]
    most = clusters * nodes // TILE
    unit = max(2, 16 * lax.axis_size("feat") // TILE)
    buckets = [b for b in BUCKETS if b < most and b % unit == 0] + [most]
    ordered = sorted(buckets)
    branch = jnp.int32(buckets.index(ordered[0]))
    for low, high in zip(ordered, ordered[1:]):
        branch = jnp.where(need > low, buckets.index(high), branch)
    branches = [functools.partial(run, b) for b in buckets]
    args = (features, adjacency, counts, offsets, weight, bias, cotangent)
    activations, grad_features, grad_weight, grad_bias = lax.switch(branch, branches, *args)
    return (
        activations.transpose(1, 0, 2),
        grad_features.transpose(1, 0, 2),
        grad_weight,
        grad_bias,
    )


def solution(mesh):
    placed = (
        P("feat", "rep", None),
        P("rep", None, None),
        P("rep"),
        P(),
        P(),
        P("feat", "rep", None),
    )
    return jax.shard_map(
        local,
        mesh=mesh,
        in_specs=placed,
        out_specs=(P("feat", "rep", None), P("feat", "rep", None), P(), P()),
        check_vma=False,
    )
```

```python
import functools

import jax
import jax.numpy as jnp
from jax import lax
from jax.experimental import pallas as pl
from jax.experimental.pallas import tpu as pltpu
from jax.sharding import PartitionSpec as P

TILE = 128
ROWS = 512
SIDE = 512
OUTER = 4
SLAB = 128
DEEP = 512
CHUNKS = 2
F32 = jnp.float32
BF16 = jnp.bfloat16
BUCKETS = (64,)


def params(mib=60):
    return pltpu.CompilerParams(vmem_limit_bytes=mib * 1024 * 1024)


def cost(flops, moved, transcendentals=0):
    return pl.CostEstimate(flops=flops, bytes_accessed=moved, transcendentals=transcendentals)


def dot(a, b, ca, cb):
    return lax.dot_general(a, b, (((ca,), (cb,)), ((), ())), preferred_element_type=F32)


def anywhere(values):
    return [pl.BlockSpec(memory_space=pl.ANY) for _ in values]


def eye():
    row = lax.broadcasted_iota(jnp.int32, (TILE, TILE), 0)
    return row == lax.broadcasted_iota(jnp.int32, (TILE, TILE), 1)


def aligned(index, size=TILE):
    return pl.ds(pl.multiple_of(index * TILE, TILE), size)


def by_groups(first, last, one, size=4):
    groups = (last - first) // size

    def group(n, carry):
        for k in range(size):
            one(first + n * size + k)
        return carry

    def single(t, carry):
        one(t)
        return carry

    lax.fori_loop(0, groups, group, 0)
    lax.fori_loop(first + groups * size, last, single, 0)


def clear_tail(out_ref, first, last):
    def one(p):
        out_ref[aligned(p), :] = jnp.zeros((TILE, out_ref.shape[1]), out_ref.dtype)

    by_groups(first, last, one)


def pack_kernel(clusters, counts, offsets, in_ref, out_ref):
    features = in_ref.shape[1]
    for c in range(clusters):
        live = counts[c]
        start = offsets[c]

        def one(t):
            lane = t * TILE + lax.broadcasted_iota(jnp.int32, (features, TILE), 1)
            block = jnp.where(lane < live, in_ref[c, :, aligned(t)].astype(F32), 0.0)
            out_ref[aligned(start + t), :] = block.T.astype(out_ref.dtype)

        by_groups(0, offsets[c + 1] - start, one)
    clear_tail(out_ref, offsets[clusters], out_ref.shape[0] // TILE)


def pack(tiles, counts, offsets, values):
    clusters, features, nodes = values.shape
    size = tiles * TILE * features
    return pl.pallas_call(
        functools.partial(pack_kernel, clusters),
        name="pack",
        out_shape=jax.ShapeDtypeStruct((tiles * TILE, features), BF16),
        grid_spec=pltpu.PrefetchScalarGridSpec(
            num_scalar_prefetch=2,
            grid=(1,),
            in_specs=[pl.BlockSpec((clusters, features, nodes), lambda i, *_: (0, 0, 0))],
            out_specs=pl.BlockSpec((tiles * TILE, features), lambda i, *_: (0, 0)),
        ),
        compiler_params=params(16),
        cost_estimate=cost(size, 4 * size),
    )(counts, offsets, values)


def unpack_kernel(count, counts, offsets, me, *refs):
    out_ref, packed = refs[-2:]
    c = pl.program_id(0)
    features = out_ref.shape[1]
    live = counts[c]
    start = offsets[c]

    @pl.when(c == 0)
    def _():
        blocks = [(k, low, refs[low].at[k]) for low in range(count) for k in range(OUTER)]
        gather_rows(me[0], count, blocks, packed)

    def one(t):
        lane = t * TILE + lax.broadcasted_iota(jnp.int32, (features, TILE), 1)
        block = packed[aligned(start + t), :].astype(F32).T
        out_ref[0, :, aligned(t)] = jnp.where(lane < live, block, 0.0)

    def clear(t):
        out_ref[0, :, aligned(t)] = jnp.zeros((features, TILE), F32)

    used = offsets[c + 1] - start
    by_groups(0, used, one)
    by_groups(used, out_ref.shape[2] // TILE, clear)


def unpack(shape, counts, offsets, me, values, after=()):
    clusters, features, nodes = shape
    count = len(values)
    size = count * values[0].size
    whole = pl.BlockSpec(values[0].shape, lambda c, *_: (0, 0, 0))
    return pl.pallas_call(
        functools.partial(unpack_kernel, count),
        name="unpack",
        out_shape=jax.ShapeDtypeStruct(shape, F32),
        grid_spec=pltpu.PrefetchScalarGridSpec(
            num_scalar_prefetch=3,
            grid=(clusters,),
            in_specs=[whole] * count + anywhere(after),
            out_specs=pl.BlockSpec((1, features, nodes), lambda c, *_: (c, 0, 0)),
            scratch_shapes=[pltpu.VMEM((size // features, features), BF16)],
        ),
        compiler_params=params(16),
        cost_estimate=cost(size, 2 * size + 4 * clusters * features * nodes),
    )(counts, offsets, me, *values, *after)


def adjacency_spec(nodes):
    def index(c, i, counts, offsets):
        return (c, jnp.minimum(i, (counts[c] - 1) // ROWS), 0)

    return pl.BlockSpec((1, ROWS, nodes), index)


def aggregate_kernel(clusters, counts, offsets, x_ref, a_ref, *refs):
    out_ref, masked = refs[-2:]
    c = pl.program_id(0)
    i = pl.program_id(1)
    live = counts[c]

    @pl.when(jnp.logical_and(c == 0, i == 0))
    def _():
        clear_tail(out_ref, offsets[clusters], out_ref.shape[0] // TILE)

    @pl.when(i == 0)
    def _():
        lane = lax.broadcasted_iota(jnp.int32, masked.shape, 1)
        masked[...] = jnp.where(lane < live, x_ref[0].astype(F32), 0.0).astype(BF16)

    @pl.when(i * ROWS < live)
    def _():
        total = dot(a_ref[0], masked[...], 1, 1)
        for s in range(ROWS // TILE):
            t = i * (ROWS // TILE) + s

            @pl.when(t * TILE < live)
            def _():
                block = a_ref[0, s * TILE : (s + 1) * TILE, aligned(t)]
                block = jnp.where(eye(), block.astype(F32), 0.0).astype(BF16)
                extra = dot(block, masked[:, aligned(t)], 1, 1)
                rows = total[s * TILE : (s + 1) * TILE] + extra
                out_ref[aligned(offsets[c] + t), :] = rows.astype(BF16)


def aggregate(tiles, counts, offsets, features, adjacency, after):
    clusters, width, nodes = features.shape
    return pl.pallas_call(
        functools.partial(aggregate_kernel, clusters),
        name="aggregate",
        out_shape=jax.ShapeDtypeStruct((tiles * TILE, width), BF16),
        grid_spec=pltpu.PrefetchScalarGridSpec(
            num_scalar_prefetch=2,
            grid=(clusters, nodes // ROWS),
            in_specs=[
                pl.BlockSpec((1, width, nodes), lambda c, i, *_: (c, 0, 0)),
                adjacency_spec(nodes),
                *anywhere((after,)),
            ],
            out_specs=pl.BlockSpec((tiles * TILE, width), lambda c, i, *_: (0, 0)),
            scratch_shapes=[pltpu.VMEM((width, nodes), BF16)],
        ),
        compiler_params=params(16),
        cost_estimate=cost(2 * adjacency.size * width, 2 * adjacency.size),
    )(counts, offsets, features, adjacency, after)


def spread_kernel(clusters, counts, offsets, packed, a_ref, *refs):
    out_ref, turned, held, sems = refs[-4:]
    c = pl.program_id(0)
    slot = lax.rem(c, 2)
    live = counts[c]
    width, nodes = turned.shape
    sizes = range(SIDE, nodes + SIDE, SIDE)

    def each(cluster, act):
        need = counts[cluster]
        for size in sizes:

            @pl.when(jnp.logical_and(need > size - SIDE, need <= size))
            def _():
                act(size)

    def copy(cluster, place, size):
        area = (slice(0, size), slice(0, size))
        return pltpu.make_async_copy(
            a_ref.at[(cluster, *area)], held.at[(place, *area)], sems.at[place]
        )

    @pl.when(c == 0)
    def _():
        each(c, lambda size: copy(c, slot, size).start())

    @pl.when(c + 1 < clusters)
    def _():
        each(c + 1, lambda size: copy(c + 1, 1 - slot, size).start())

    start = offsets[c]
    used = offsets[c + 1] - start

    def turn(t):
        lane = t * TILE + lax.broadcasted_iota(jnp.int32, (width, TILE), 1)
        block = packed[aligned(start + t), :].astype(F32).T
        turned[:, aligned(t)] = jnp.where(lane < live, block, 0.0).astype(BF16)

    def clear(t):
        turned[:, aligned(t)] = jnp.zeros((width, TILE), BF16)

    by_groups(0, used, turn)
    by_groups(used, nodes // TILE, clear)

    def compute(size):
        copy(c, slot, size).wait()

        def columns(n, carry):
            j = n * (SIDE // TILE)
            total = dot(turned[:, :size], held[slot, :size, aligned(j, SIDE)], 1, 0)
            for k in range(SIDE // TILE):
                here = aligned(j + k)
                rows = pl.ds(pl.multiple_of((j + k) * TILE, TILE), TILE)
                block = held[slot, rows, here].astype(F32)
                diagonal = jnp.sum(jnp.where(eye(), block, 0.0), axis=0, keepdims=True)
                extra = diagonal * turned[:, here].astype(F32)
                lane = (j + k) * TILE + lax.broadcasted_iota(jnp.int32, (width, TILE), 1)
                value = total[:, k * TILE : (k + 1) * TILE] + extra
                out_ref[0, :, here] = jnp.where(lane < live, value, 0.0)
            return carry

        lax.fori_loop(0, size // SIDE, columns, 0)
        if size < nodes:
            out_ref[0, :, size:] = jnp.zeros((width, nodes - size), F32)

    each(c, compute)


def spread(counts, offsets, packed, adjacency, after=()):
    clusters, nodes, _ = adjacency.shape
    width = packed.shape[1]
    return pl.pallas_call(
        functools.partial(spread_kernel, clusters),
        name="spread",
        out_shape=jax.ShapeDtypeStruct((clusters, width, nodes), F32),
        grid_spec=pltpu.PrefetchScalarGridSpec(
            num_scalar_prefetch=2,
            grid=(clusters,),
            in_specs=[pl.BlockSpec(packed.shape, lambda c, *_: (0, 0))]
            + anywhere((adjacency, *after)),
            out_specs=pl.BlockSpec((1, width, nodes), lambda c, *_: (c, 0, 0)),
            scratch_shapes=[
                pltpu.VMEM((width, nodes), BF16),
                pltpu.VMEM((2, nodes, nodes), BF16),
                pltpu.SemaphoreType.DMA((2,)),
            ],
        ),
        compiler_params=params(32),
        cost_estimate=cost(2 * adjacency.size * width, 2 * adjacency.size),
    )(counts, offsets, packed, adjacency, *after)


def normal(value):
    bell = jnp.exp(-0.5 * value * value)
    t = 1.0 / (1.0 + (0.3275911 * 0.5**0.5) * jnp.abs(value))
    tail = 0.5 * 1.061405429
    for term in (-1.453152027, 1.421413741, -0.284496736, 0.254829592):
        tail = tail * t + 0.5 * term
    tail = tail * t * bell
    return jnp.where(value >= 0.0, 1.0 - tail, tail), bell * 0.3989422804014327


def middle_kernel(me, agg_ref, cot_ref, w_ref, b_ref, act_ref, low_ref, bias_ref, held, product):
    owners, rows, width = agg_ref.shape

    @pl.when(pl.program_id(0) == 0)
    def _():
        for s in range(owners):
            held[:, s * width : (s + 1) * width] = agg_ref[s]

    parts = cot_ref.shape[0]
    product[...] = dot(held[...], w_ref[...], 1, 0)
    step = max(n for n in range(16, SLAB + 16, 16) if rows % n == 0)

    def slab(n, total):
        some = pl.ds(pl.multiple_of(n * step, 16), step)
        pre = product[some] + b_ref[...].astype(F32)
        cdf, pdf = normal(pre)
        act = (pre * cdf).astype(BF16)
        cot = jnp.concatenate([cot_ref[k, some] for k in range(parts)], axis=1).astype(F32)
        grad = cot * (cdf + pre * pdf)
        for k in range(parts):
            act_ref[0, k ^ me[0], some] = act[:, k * width : (k + 1) * width]
        low_ref[some] = grad.astype(BF16)
        return total + jnp.sum(grad, axis=0, keepdims=True)

    bias_ref[...] = lax.fori_loop(0, rows // step, slab, jnp.zeros((1, w_ref.shape[1]), F32))


def middle(me, agg, cot, weight, bias):
    owners, rows, width = agg.shape
    full = owners * width
    inner = owners // OUTER
    block = inner * width
    return pl.pallas_call(
        middle_kernel,
        name="middle",
        out_shape=(
            jax.ShapeDtypeStruct((OUTER, inner, rows, width), BF16),
            jax.ShapeDtypeStruct((rows, full), BF16),
            jax.ShapeDtypeStruct((1, full), F32),
        ),
        grid_spec=pltpu.PrefetchScalarGridSpec(
            num_scalar_prefetch=1,
            grid=(OUTER,),
            in_specs=[
                pl.BlockSpec((owners, rows, width), lambda g, me: (0, 0, 0)),
                pl.BlockSpec((inner, rows, width), lambda g, me: (g, 0, 0)),
                pl.BlockSpec((full, block), lambda g, me: (0, g)),
                pl.BlockSpec((1, block), lambda g, me: (0, g)),
            ],
            out_specs=(
                pl.BlockSpec((1, inner, rows, width), lambda g, me: (g, 0, 0, 0)),
                pl.BlockSpec((rows, block), lambda g, me: (0, g)),
                pl.BlockSpec((1, block), lambda g, me: (0, g)),
            ),
            scratch_shapes=[pltpu.VMEM((rows, full), BF16), pltpu.VMEM((rows, block), F32)],
        ),
        compiler_params=params(28),
        cost_estimate=cost(2 * rows * full * full, 2 * full * full + 8 * rows * full),
    )(me, agg, cot, weight, bias[None])


def turned_dot(agg_ref, low_ref):
    left = jnp.concatenate([agg_ref[s].T for s in range(agg_ref.shape[0])], axis=0)
    return dot(left, low_ref[...], 1, 0)


def clamped(i, first, count):
    return jnp.clip(i - first, 0, count - 1)


def outer_kernel(blocks, which, agg_ref, low_ref, *out_refs):
    for k, out_ref in enumerate(out_refs):

        @pl.when(pl.program_id(0) // blocks == k)
        def _():
            out_ref[...] = turned_dot(agg_ref, low_ref).astype(BF16)


def outer(which, agg, low):
    owners, rows, width = agg.shape
    full = owners * width
    step = DEEP
    share = full // CHUNKS
    blocks = share // step

    def target(k):
        return lambda i, which: (clamped(i, k * blocks, blocks), 0)

    return pl.pallas_call(
        functools.partial(outer_kernel, blocks),
        name="outer",
        out_shape=[jax.ShapeDtypeStruct((share, full // 2), BF16)] * CHUNKS,
        grid_spec=pltpu.PrefetchScalarGridSpec(
            num_scalar_prefetch=1,
            grid=(CHUNKS * blocks,),
            in_specs=[
                pl.BlockSpec((step // width, rows, width), lambda i, which: (i, 0, 0)),
                pl.BlockSpec((rows, full // 2), lambda i, which: (0, which[0])),
            ],
            out_specs=[pl.BlockSpec((step, full // 2), target(k)) for k in range(CHUNKS)],
        ),
        compiler_params=params(20),
        cost_estimate=cost(rows * full * full, 4 * rows * full + full * full),
    )(which[None].astype(jnp.int32), agg, low)


def outer_halve_kernel(blocks, which, agg_ref, low_ref, *refs):
    i = pl.program_id(0)
    outs = refs[-2 * CHUNKS :]
    for n, out_ref in enumerate(outs):
        came_ref = refs[n // 2]

        @pl.when(i // blocks == n)
        def _():
            total = turned_dot(agg_ref, low_ref) + came_ref[...].astype(F32)
            out_ref[...] = total.astype(out_ref.dtype)


def outer_halve(which, side, agg, low, came, after=()):
    owners, rows, width = agg.shape
    full = owners * width
    step = DEEP
    half = full // CHUNKS // 2
    blocks = half // step

    def row(i, which):
        k = i // (2 * blocks)
        part = i // blocks % 2
        near = jnp.where(k == 0, which[1], which[2])
        return k * 2 * blocks + jnp.where(part == 0, 1 - near, near) * blocks + i % blocks

    def arrived(k):
        def index(i, which):
            inside = clamped(i, k * 2 * blocks, 2 * blocks) + k * 2 * blocks
            return (row(inside, which) - k * 2 * blocks, 0)

        return index

    def target(n):
        return lambda i, which: (clamped(i, n * blocks, blocks), 0)

    outs = pl.pallas_call(
        functools.partial(outer_halve_kernel, blocks),
        name="outer_halve",
        out_shape=[
            jax.ShapeDtypeStruct((half, full // 2), dtype) for dtype in (BF16, F32) * CHUNKS
        ],
        grid_spec=pltpu.PrefetchScalarGridSpec(
            num_scalar_prefetch=1,
            grid=(2 * CHUNKS * blocks,),
            in_specs=[
                pl.BlockSpec(
                    (step // width, rows, width), lambda i, which: (row(i, which), 0, 0)
                ),
                pl.BlockSpec((rows, full // 2), lambda i, which: (0, which[0])),
            ]
            + [pl.BlockSpec((step, full // 2), arrived(k)) for k in range(CHUNKS)]
            + anywhere(after),
            out_specs=[pl.BlockSpec((step, full // 2), target(n)) for n in range(2 * CHUNKS)],
        ),
        compiler_params=params(28),
        cost_estimate=cost(rows * full * full, 4 * rows * full + 4 * full * full),
    )(jnp.stack([which, *side]).astype(jnp.int32), agg, low, *came, *after)
    return outs[0::2], outs[1::2]


def back_kernel(low_ref, w_ref, *refs):
    out_ref = refs[-1]
    parts, _, width = out_ref.shape
    value = dot(low_ref[...], w_ref[...], 1, 1).astype(BF16)
    for k in range(parts):
        out_ref[k] = value[:, k * width : (k + 1) * width]


def back(low, weight, owners, after=()):
    rows, full = low.shape
    width = full // owners
    step = DEEP
    return pl.pallas_call(
        back_kernel,
        name="back",
        out_shape=jax.ShapeDtypeStruct((owners, rows, width), BF16),
        grid=(full // step,),
        in_specs=[
            pl.BlockSpec((rows, full), lambda i: (0, 0)),
            pl.BlockSpec((step, full), lambda i: (i, 0)),
        ]
        + anywhere(after),
        out_specs=pl.BlockSpec((step // width, rows, width), lambda i: (i, 0, 0)),
        compiler_params=params(20),
        cost_estimate=cost(2 * rows * full * full, 2 * full * full + 4 * rows * full),
    )(low, weight, *after)


def split_kernel(value_ref, *refs):
    count = value_ref.shape[1]
    for j, out_ref in enumerate(refs[-count:]):
        out_ref[...] = value_ref[:, j]


def row_step(rows):
    return rows // 2 if rows % 32 == 0 else rows


def split(value, after=()):
    first, second, rows, width = value.shape
    step = row_step(rows)
    return pl.pallas_call(
        split_kernel,
        name="split",
        out_shape=[jax.ShapeDtypeStruct((first, rows, width), BF16)] * second,
        grid=(rows // step,),
        in_specs=[pl.BlockSpec((first, second, step, width), lambda i: (0, 0, i, 0))]
        + anywhere(after),
        out_specs=[pl.BlockSpec((first, step, width), lambda i: (0, i, 0))] * second,
        compiler_params=params(16),
        cost_estimate=cost(0, 4 * value.size),
    )(value, *after)


def swap_with(value, mask):
    count = lax.axis_size("feat")
    return lax.ppermute(value, "feat", [(i, i ^ mask) for i in range(count)])


def scatter(values):
    return [values[0]] + [swap_with(values[k], k) for k in range(1, len(values))]


def outer_exchange(value):
    inner = lax.axis_size("feat") // OUTER
    groups = [[k * inner + low for k in range(OUTER)] for low in range(inner)]
    return lax.all_to_all(
        value, "feat", split_axis=0, concat_axis=0, axis_index_groups=groups, tiled=True
    )


def gather_rows(me, inner, blocks, out_ref):
    for high, low, block in blocks:
        rows = block.shape[0]
        owner = high * inner + (me ^ low)
        out_ref[pl.ds(pl.multiple_of(owner * rows, 16), rows), :] = block[...]


def swap_feat(value, bit):
    return swap_with(value, 1 << bit)


def swap_rep(value):
    return lax.ppermute(value, "rep", [(0, 1), (1, 0)])


def exchange(packed):
    owners = lax.axis_size("feat")
    blocks = packed.reshape(owners, -1, packed.shape[-1])
    return lax.all_to_all(blocks, "feat", split_axis=0, concat_axis=0, tiled=True)


def place_kernel(count, where, *refs):
    out_ref = refs[-1]
    for k in range(count):

        @pl.when(pl.program_id(0) == k)
        def _():
            out_ref[...] = refs[k][...].astype(F32)


def place(where, pieces, before=None, after=()):
    count = len(pieces)
    rows, columns = pieces[0].shape
    step = min(rows, 512)
    steps = rows // step
    full = 2 * columns
    begun = () if before is None else (before,)

    def source(k):
        return lambda i, j, where: (jnp.where(i == k, j, jnp.where(i < k, 0, steps - 1)), 0)

    return pl.pallas_call(
        functools.partial(place_kernel, count),
        name="place",
        out_shape=jax.ShapeDtypeStruct((full, full), F32),
        grid_spec=pltpu.PrefetchScalarGridSpec(
            num_scalar_prefetch=1,
            grid=(count, steps),
            in_specs=[pl.BlockSpec((step, columns), source(k)) for k in range(count)]
            + anywhere(begun)
            + anywhere(after),
            out_specs=pl.BlockSpec(
                (step, columns), lambda i, j, where: (where[i] * steps + j, where[count + i])
            ),
        ),
        input_output_aliases={1 + count: 0} if begun else {},
        compiler_params=params(16),
        cost_estimate=cost(0, 6 * count * rows * columns),
    )(jnp.stack(where).astype(jnp.int32), *pieces, *begun, *after)


def halve_kernel(chunks, side, *refs):
    outs = refs[-2 * chunks :]
    for k in range(chunks):
        for part in range(2):
            kept, came = refs[4 * k + 2 * part], refs[4 * k + 2 * part + 1]
            out = outs[2 * k + part]
            out[...] = (kept[...].astype(F32) + came[...].astype(F32)).astype(out.dtype)


def halve(side, kept, came, after=()):
    chunks = len(kept)
    half, columns = kept[0].shape[0] // 2, kept[0].shape[1]
    step = min(half, 128)
    steps = half // step

    def source(k, part):
        return lambda i, side: ((side[k] if part else 1 - side[k]) * steps + i, 0)

    in_specs = []
    operands = []
    out_shape = []
    for k in range(chunks):
        for part in range(2):
            for value in (kept[k], came[k]):
                in_specs.append(pl.BlockSpec((step, columns), source(k, part)))
                operands.append(value)
        for dtype in (BF16, F32):
            out_shape.append(jax.ShapeDtypeStruct((half, columns), dtype))
    outs = pl.pallas_call(
        functools.partial(halve_kernel, chunks),
        name="halve",
        out_shape=tuple(out_shape),
        grid_spec=pltpu.PrefetchScalarGridSpec(
            num_scalar_prefetch=1,
            grid=(steps,),
            in_specs=in_specs + anywhere(after),
            out_specs=[pl.BlockSpec((step, columns), lambda i, side: (i, 0)) for _ in out_shape],
        ),
        compiler_params=params(16),
        cost_estimate=cost(2 * chunks * half * columns, 18 * chunks * half * columns),
    )(jnp.stack(side).astype(jnp.int32), *operands, *after)
    return outs[0::2], outs[1::2]


def pick_kernel(side, *refs):
    first, second = (refs[2 * k][...] + refs[2 * k + 1][...].astype(F32) for k in range(2))
    away_ref, own_ref = refs[-2:]

    @pl.when(side[0] == 0)
    def _():
        own_ref[...] = first
        away_ref[...] = second.astype(BF16)

    @pl.when(side[0] == 1)
    def _():
        own_ref[...] = second
        away_ref[...] = first.astype(BF16)


def pick(side, kept, came, after=()):
    rows, columns = kept[0].shape
    step = min(rows, 128)
    block = pl.BlockSpec((step, columns), lambda i, side: (i, 0))
    away, own = pl.pallas_call(
        pick_kernel,
        name="pick",
        out_shape=(
            jax.ShapeDtypeStruct((rows, columns), BF16),
            jax.ShapeDtypeStruct((rows, columns), F32),
        ),
        grid_spec=pltpu.PrefetchScalarGridSpec(
            num_scalar_prefetch=1,
            grid=(rows // step,),
            in_specs=[block] * 4 + anywhere(after),
            out_specs=(block, block),
        ),
        compiler_params=params(16),
        cost_estimate=cost(2 * rows * columns, 18 * rows * columns),
    )(side[None].astype(jnp.int32), kept[0], came[0], kept[1], came[1], *after)
    return [away], [own]


def sort_kernel(side, own_ref, other_ref, *refs):
    first_ref, second_ref = refs[-2:]

    @pl.when(side[0] == 0)
    def _():
        first_ref[...] = own_ref[...]
        second_ref[...] = other_ref[...]

    @pl.when(side[0] == 1)
    def _():
        first_ref[...] = other_ref[...]
        second_ref[...] = own_ref[...]


def sort(side, own, other, after=()):
    whole = pl.BlockSpec(own.shape, lambda i, side: (0, 0))
    return pl.pallas_call(
        sort_kernel,
        name="sort",
        out_shape=[jax.ShapeDtypeStruct(own.shape, BF16)] * 2,
        grid_spec=pltpu.PrefetchScalarGridSpec(
            num_scalar_prefetch=1,
            grid=(1,),
            in_specs=[whole, whole] + anywhere(after),
            out_specs=[whole, whole],
        ),
        compiler_params=params(16),
        cost_estimate=cost(0, 8 * own.size),
    )(side[None].astype(jnp.int32), own, other, *after)


def add_kernel(first_ref, second_ref, *refs):
    refs[-1][...] = first_ref[...] + second_ref[...]


def add(first, second, after=()):
    return pl.pallas_call(
        add_kernel,
        name="add",
        out_shape=jax.ShapeDtypeStruct(first.shape, F32),
        in_specs=[pl.BlockSpec(memory_space=pltpu.VMEM)] * 2 + anywhere(after),
        compiler_params=params(16),
        cost_estimate=cost(first.size, 12 * first.size),
    )(first, second, *after)


def close_kernel(chunks, *refs):
    for k in range(chunks):
        total = refs[2 * k][...] + refs[2 * k + 1][...].astype(F32)
        refs[len(refs) - chunks + k][...] = total.astype(BF16)


def close(kept, came, after=()):
    chunks = len(kept)
    pairs = [value for pair in zip(kept, came) for value in pair]
    return pl.pallas_call(
        functools.partial(close_kernel, chunks),
        name="close",
        out_shape=[jax.ShapeDtypeStruct(value.shape, BF16) for value in kept],
        in_specs=[pl.BlockSpec(memory_space=pltpu.VMEM) for _ in pairs] + anywhere(after),
        compiler_params=params(16),
        cost_estimate=cost(kept[0].size * chunks, 8 * kept[0].size * chunks),
    )(*pairs, *after)


def join_kernel(chunks, side, *refs):
    outs = refs[-chunks:]
    for k in range(chunks):
        for part in range(2):

            @pl.when(pl.program_id(0) == part)
            def _():
                outs[k][...] = refs[2 * k + part][...]


def join(side, own, other, after=()):
    chunks = len(own)
    rows, columns = own[0].shape
    step = min(rows, 256)
    steps = rows // step
    pairs = [value for pair in zip(own, other) for value in pair]

    def source(part):
        return lambda i, j, side: (jnp.where(i == part, j, 0 if part else steps - 1), 0)

    def target(k):
        return lambda i, j, side: (jnp.where(i == 0, side[k], 1 - side[k]) * steps + j, 0)

    return pl.pallas_call(
        functools.partial(join_kernel, chunks),
        name="join",
        out_shape=[jax.ShapeDtypeStruct((2 * rows, columns), BF16) for _ in own],
        grid_spec=pltpu.PrefetchScalarGridSpec(
            num_scalar_prefetch=1,
            grid=(2, steps),
            in_specs=[pl.BlockSpec((step, columns), source(n % 2)) for n in range(2 * chunks)]
            + anywhere(after),
            out_specs=[pl.BlockSpec((step, columns), target(k)) for k in range(chunks)],
        ),
        compiler_params=params(16),
        cost_estimate=cost(0, 8 * chunks * rows * columns),
    )(jnp.stack(side).astype(jnp.int32), *pairs, *after)


def run(tiles, features, adjacency, counts, offsets, weight, bias, cotangent):
    owners = lax.axis_size("feat")
    me = lax.axis_index("feat")
    core = lax.axis_index("rep")
    bits = owners.bit_length() - 1
    inner = owners // OUTER
    side = [(me >> bit) & 1 for bit in range(bits)]
    crossed = [1, 0]
    low_bits = (me & (inner - 1)).astype(jnp.int32)
    place_of = low_bits[None]

    cot = pack(tiles, counts, offsets, cotangent)
    agg = exchange(aggregate(tiles, counts, offsets, features, adjacency, cot))
    cot = exchange(cot)
    act, low, grad_bias = middle(place_of, agg, cot, weight, bias)
    sent = outer(1 - core, agg, low)
    came = [swap_rep(value) for value in sent]
    act, _ = lax.optimization_barrier((act, sent[0]))
    act = outer_exchange(act)

    came_bias = swap_rep(grad_bias)
    away, kept = outer_halve(core, side[:2], agg, low, came)
    came = [swap_feat(away[k], k) for k in range(2)]
    back_rows = back(low, weight, owners, away)
    grad_bias = add(grad_bias, came_bias, (back_rows,))
    came_bias = swap_feat(grad_bias, 0)
    away, kept = halve([side[1], side[0]], kept, came, (grad_bias,))
    came = [swap_feat(away[k], crossed[k]) for k in range(2)]
    grad_bias = add(grad_bias, came_bias, away)
    came_bias = swap_feat(grad_bias, 1)
    away, kept = pick(side[2], kept, came, (grad_bias,))
    came = [swap_feat(away[0], 2)]
    act = split(act, away)
    grad_bias = add(grad_bias, came_bias, (act[0],))
    act = scatter(act)
    for bit in range(3, bits):
        came_bias = swap_feat(grad_bias, bit - 1)
        away, kept = halve(side[bit : bit + 1], kept, came, (grad_bias,))
        came = [swap_feat(away[0], bit)]
        grad_bias = add(grad_bias, came_bias, away)
    came_bias = swap_feat(grad_bias, bits - 1)
    grad_bias = add(grad_bias, came_bias, away)
    owned = close(kept, came, (grad_bias,))
    for bit in reversed(range(3, bits)):
        owned = join(side[bit : bit + 1], owned, [swap_feat(owned[0], bit)])
    other = swap_feat(owned[0], 2)
    activations = unpack(features.shape, counts, offsets, place_of, act, owned)
    owned = sort(side[2], owned[0], other, (activations,))
    other = [swap_feat(owned[k], crossed[k]) for k in range(2)]
    back_rows, owned = lax.optimization_barrier((back_rows, owned))
    back_rows = exchange(back_rows).reshape(tiles * TILE, -1)
    owned = join([side[1], side[0]], owned, other)
    across = [swap_rep(value) for value in owned]
    far = [swap_feat(owned[k], k) for k in range(2)]
    near_rows = [2 * k + side[k] for k in range(2)]
    far_rows = [2 * k + 1 - side[k] for k in range(2)]
    columns = [core] * 2 + [1 - core] * 2
    grad_weight = place(2 * near_rows + columns, [*owned, *across])
    grad_features = spread(counts, offsets, back_rows, adjacency, (grad_weight,))
    far, grad_features = lax.optimization_barrier((far, grad_features))
    far_across = [swap_rep(value) for value in far]
    grad_weight = place(far_rows + columns[:2], far, grad_weight)
    grad_weight = place(far_rows + columns[2:], far_across, grad_weight)
    return activations, grad_features, grad_weight, grad_bias[0]


def local(features, adjacency, counts, weight, bias, cotangent):
    features = features.transpose(1, 0, 2)
    cotangent = cotangent.transpose(1, 0, 2)
    clusters, _, nodes = features.shape
    used = (counts + TILE - 1) // TILE
    before = jnp.arange(clusters)[None] < jnp.arange(clusters + 1)[:, None]
    offsets = jnp.sum(jnp.where(before, used[None], 0), axis=1).astype(jnp.int32)
    need = offsets[-1:]
    need = jnp.maximum(need, swap_rep(need))[0]
    most = clusters * nodes // TILE
    unit = max(2, 16 * lax.axis_size("feat") // TILE)
    buckets = [b for b in BUCKETS if b < most and b % unit == 0] + [most]
    ordered = sorted(buckets)
    branch = jnp.int32(buckets.index(ordered[0]))
    for low, high in zip(ordered, ordered[1:]):
        branch = jnp.where(need > low, buckets.index(high), branch)
    branches = [functools.partial(run, b) for b in buckets]
    args = (features, adjacency, counts, offsets, weight, bias, cotangent)
    activations, grad_features, grad_weight, grad_bias = lax.switch(branch, branches, *args)
    return (
        activations.transpose(1, 0, 2),
        grad_features.transpose(1, 0, 2),
        grad_weight,
        grad_bias,
    )


def solution(mesh):
    placed = (
        P("feat", "rep", None),
        P("rep", None, None),
        P("rep"),
        P(),
        P(),
        P("feat", "rep", None),
    )
    return jax.shard_map(
        local,
        mesh=mesh,
        in_specs=placed,
        out_specs=(P("feat", "rep", None), P("feat", "rep", None), P(), P()),
        check_vma=False,
    )
```

```python
import functools

import jax
import jax.numpy as jnp
from jax import lax
from jax.experimental import pallas as pl
from jax.experimental.pallas import tpu as pltpu
from jax.sharding import PartitionSpec as P

TILE = 128
ROWS = 512
SIDE = 512
OUTER = 4
SLAB = 128
DEEP = 512
CHUNKS = 2
F32 = jnp.float32
BF16 = jnp.bfloat16
BUCKETS = (60, 70)


def params(mib=60):
    return pltpu.CompilerParams(vmem_limit_bytes=mib * 1024 * 1024)


def cost(flops, moved, transcendentals=0):
    return pl.CostEstimate(flops=flops, bytes_accessed=moved, transcendentals=transcendentals)


def dot(a, b, ca, cb):
    return lax.dot_general(a, b, (((ca,), (cb,)), ((), ())), preferred_element_type=F32)


def anywhere(values):
    return [pl.BlockSpec(memory_space=pl.ANY) for _ in values]


def eye():
    row = lax.broadcasted_iota(jnp.int32, (TILE, TILE), 0)
    return row == lax.broadcasted_iota(jnp.int32, (TILE, TILE), 1)


def aligned(index, size=TILE):
    return pl.ds(pl.multiple_of(index * TILE, TILE), size)


def by_groups(first, last, one, size=4):
    groups = (last - first) // size

    def group(n, carry):
        for k in range(size):
            one(first + n * size + k)
        return carry

    def single(t, carry):
        one(t)
        return carry

    lax.fori_loop(0, groups, group, 0)
    lax.fori_loop(first + groups * size, last, single, 0)


def clear_tail(out_ref, first, last):
    def one(p):
        out_ref[aligned(p), :] = jnp.zeros((TILE, out_ref.shape[1]), out_ref.dtype)

    by_groups(first, last, one)


def pack_kernel(clusters, counts, offsets, in_ref, out_ref):
    features = in_ref.shape[1]

    def cluster(c, carry):
        live = counts[c]
        start = offsets[c]

        def one(t):
            lane = t * TILE + lax.broadcasted_iota(jnp.int32, (features, TILE), 1)
            block = jnp.where(lane < live, in_ref[c, :, aligned(t)].astype(F32), 0.0)
            out_ref[aligned(start + t), :] = block.T.astype(out_ref.dtype)

        by_groups(0, offsets[c + 1] - start, one)
        return carry

    lax.fori_loop(0, clusters, cluster, 0)
    clear_tail(out_ref, offsets[clusters], out_ref.shape[0] // TILE)


def pack(tiles, counts, offsets, values):
    clusters, features, nodes = values.shape
    size = tiles * TILE * features
    return pl.pallas_call(
        functools.partial(pack_kernel, clusters),
        name="pack",
        out_shape=jax.ShapeDtypeStruct((tiles * TILE, features), BF16),
        grid_spec=pltpu.PrefetchScalarGridSpec(
            num_scalar_prefetch=2,
            grid=(1,),
            in_specs=[pl.BlockSpec((clusters, features, nodes), lambda i, *_: (0, 0, 0))],
            out_specs=pl.BlockSpec((tiles * TILE, features), lambda i, *_: (0, 0)),
        ),
        compiler_params=params(16),
        cost_estimate=cost(size, 4 * size),
    )(counts, offsets, values)


def unpack_kernel(count, counts, offsets, me, *refs):
    out_ref, packed = refs[-2:]
    c = pl.program_id(0)
    features = out_ref.shape[1]
    live = counts[c]
    start = offsets[c]

    @pl.when(c == 0)
    def _():
        blocks = [(k, low, refs[low].at[k]) for low in range(count) for k in range(OUTER)]
        gather_rows(me[0], count, blocks, packed)

    def one(t):
        lane = t * TILE + lax.broadcasted_iota(jnp.int32, (features, TILE), 1)
        block = packed[aligned(start + t), :].astype(F32).T
        out_ref[0, :, aligned(t)] = jnp.where(lane < live, block, 0.0)

    def clear(t):
        out_ref[0, :, aligned(t)] = jnp.zeros((features, TILE), F32)

    used = offsets[c + 1] - start
    by_groups(0, used, one)
    by_groups(used, out_ref.shape[2] // TILE, clear)


def unpack(shape, counts, offsets, me, values, after=()):
    clusters, features, nodes = shape
    count = len(values)
    size = count * values[0].size
    whole = pl.BlockSpec(values[0].shape, lambda c, *_: (0, 0, 0))
    return pl.pallas_call(
        functools.partial(unpack_kernel, count),
        name="unpack",
        out_shape=jax.ShapeDtypeStruct(shape, F32),
        grid_spec=pltpu.PrefetchScalarGridSpec(
            num_scalar_prefetch=3,
            grid=(clusters,),
            in_specs=[whole] * count + anywhere(after),
            out_specs=pl.BlockSpec((1, features, nodes), lambda c, *_: (c, 0, 0)),
            scratch_shapes=[pltpu.VMEM((size // features, features), BF16)],
        ),
        compiler_params=params(16),
        cost_estimate=cost(size, 2 * size + 4 * clusters * features * nodes),
    )(counts, offsets, me, *values, *after)


def adjacency_spec(nodes):
    def index(c, i, counts, offsets):
        return (c, jnp.minimum(i, (counts[c] - 1) // ROWS), 0)

    return pl.BlockSpec((1, ROWS, nodes), index)


def aggregate_kernel(clusters, counts, offsets, x_ref, a_ref, *refs):
    out_ref, masked = refs[-2:]
    c = pl.program_id(0)
    i = pl.program_id(1)
    live = counts[c]

    @pl.when(jnp.logical_and(c == 0, i == 0))
    def _():
        clear_tail(out_ref, offsets[clusters], out_ref.shape[0] // TILE)

    @pl.when(i == 0)
    def _():
        lane = lax.broadcasted_iota(jnp.int32, masked.shape, 1)
        masked[...] = jnp.where(lane < live, x_ref[0].astype(F32), 0.0).astype(BF16)

    @pl.when(i * ROWS < live)
    def _():
        total = dot(a_ref[0], masked[...], 1, 1)
        for s in range(ROWS // TILE):
            t = i * (ROWS // TILE) + s

            @pl.when(t * TILE < live)
            def _():
                block = a_ref[0, s * TILE : (s + 1) * TILE, aligned(t)]
                block = jnp.where(eye(), block.astype(F32), 0.0).astype(BF16)
                extra = dot(block, masked[:, aligned(t)], 1, 1)
                rows = total[s * TILE : (s + 1) * TILE] + extra
                out_ref[aligned(offsets[c] + t), :] = rows.astype(BF16)


def aggregate(tiles, counts, offsets, features, adjacency, after):
    clusters, width, nodes = features.shape
    return pl.pallas_call(
        functools.partial(aggregate_kernel, clusters),
        name="aggregate",
        out_shape=jax.ShapeDtypeStruct((tiles * TILE, width), BF16),
        grid_spec=pltpu.PrefetchScalarGridSpec(
            num_scalar_prefetch=2,
            grid=(clusters, nodes // ROWS),
            in_specs=[
                pl.BlockSpec((1, width, nodes), lambda c, i, *_: (c, 0, 0)),
                adjacency_spec(nodes),
                *anywhere((after,)),
            ],
            out_specs=pl.BlockSpec((tiles * TILE, width), lambda c, i, *_: (0, 0)),
            scratch_shapes=[pltpu.VMEM((width, nodes), BF16)],
        ),
        compiler_params=params(16),
        cost_estimate=cost(2 * adjacency.size * width, 2 * adjacency.size),
    )(counts, offsets, features, adjacency, after)


def spread_kernel(clusters, counts, offsets, packed, a_ref, *refs):
    out_ref, turned, held, sems = refs[-4:]
    c = pl.program_id(0)
    slot = lax.rem(c, 2)
    live = counts[c]
    width, nodes = turned.shape
    sizes = range(SIDE, nodes + SIDE, SIDE)

    def each(cluster, act):
        need = counts[cluster]
        for size in sizes:

            @pl.when(jnp.logical_and(need > size - SIDE, need <= size))
            def _():
                act(size)

    def copy(cluster, place, size):
        area = (slice(0, size), slice(0, size))
        return pltpu.make_async_copy(
            a_ref.at[(cluster, *area)], held.at[(place, *area)], sems.at[place]
        )

    @pl.when(c == 0)
    def _():
        each(c, lambda size: copy(c, slot, size).start())

    @pl.when(c + 1 < clusters)
    def _():
        each(c + 1, lambda size: copy(c + 1, 1 - slot, size).start())

    start = offsets[c]
    used = offsets[c + 1] - start

    def turn(t):
        lane = t * TILE + lax.broadcasted_iota(jnp.int32, (width, TILE), 1)
        block = packed[aligned(start + t), :].astype(F32).T
        turned[:, aligned(t)] = jnp.where(lane < live, block, 0.0).astype(BF16)

    def clear(t):
        turned[:, aligned(t)] = jnp.zeros((width, TILE), BF16)

    by_groups(0, used, turn)
    by_groups(used, nodes // TILE, clear)

    def compute(size):
        copy(c, slot, size).wait()

        def columns(n, carry):
            j = n * (SIDE // TILE)
            total = dot(turned[:, :size], held[slot, :size, aligned(j, SIDE)], 1, 0)
            for k in range(SIDE // TILE):
                here = aligned(j + k)
                rows = pl.ds(pl.multiple_of((j + k) * TILE, TILE), TILE)
                block = held[slot, rows, here].astype(F32)
                diagonal = jnp.sum(jnp.where(eye(), block, 0.0), axis=0, keepdims=True)
                extra = diagonal * turned[:, here].astype(F32)
                lane = (j + k) * TILE + lax.broadcasted_iota(jnp.int32, (width, TILE), 1)
                value = total[:, k * TILE : (k + 1) * TILE] + extra
                out_ref[0, :, here] = jnp.where(lane < live, value, 0.0)
            return carry

        lax.fori_loop(0, size // SIDE, columns, 0)
        if size < nodes:
            out_ref[0, :, size:] = jnp.zeros((width, nodes - size), F32)

    each(c, compute)


def spread(counts, offsets, packed, adjacency, after=()):
    clusters, nodes, _ = adjacency.shape
    width = packed.shape[1]
    return pl.pallas_call(
        functools.partial(spread_kernel, clusters),
        name="spread",
        out_shape=jax.ShapeDtypeStruct((clusters, width, nodes), F32),
        grid_spec=pltpu.PrefetchScalarGridSpec(
            num_scalar_prefetch=2,
            grid=(clusters,),
            in_specs=[pl.BlockSpec(packed.shape, lambda c, *_: (0, 0))]
            + anywhere((adjacency, *after)),
            out_specs=pl.BlockSpec((1, width, nodes), lambda c, *_: (c, 0, 0)),
            scratch_shapes=[
                pltpu.VMEM((width, nodes), BF16),
                pltpu.VMEM((2, nodes, nodes), BF16),
                pltpu.SemaphoreType.DMA((2,)),
            ],
        ),
        compiler_params=params(32),
        cost_estimate=cost(2 * adjacency.size * width, 2 * adjacency.size),
    )(counts, offsets, packed, adjacency, *after)


def normal(value):
    bell = jnp.exp(-0.5 * value * value)
    t = 1.0 / (1.0 + (0.3275911 * 0.5**0.5) * jnp.abs(value))
    tail = 0.5 * 1.061405429
    for term in (-1.453152027, 1.421413741, -0.284496736, 0.254829592):
        tail = tail * t + 0.5 * term
    tail = tail * t * bell
    return jnp.where(value >= 0.0, 1.0 - tail, tail), bell * 0.3989422804014327


def middle_kernel(me, agg_ref, cot_ref, w_ref, b_ref, act_ref, low_ref, bias_ref, held, product):
    owners, rows, width = agg_ref.shape

    @pl.when(pl.program_id(0) == 0)
    def _():
        for s in range(owners):
            held[:, s * width : (s + 1) * width] = agg_ref[s]

    parts = cot_ref.shape[0]
    product[...] = dot(held[...], w_ref[...], 1, 0)
    step = max(n for n in range(16, SLAB + 16, 16) if rows % n == 0)

    def slab(n, total):
        some = pl.ds(pl.multiple_of(n * step, 16), step)
        pre = product[some] + b_ref[...].astype(F32)
        cdf, pdf = normal(pre)
        act = (pre * cdf).astype(BF16)
        cot = jnp.concatenate([cot_ref[k, some] for k in range(parts)], axis=1).astype(F32)
        grad = cot * (cdf + pre * pdf)
        for k in range(parts):
            act_ref[0, k ^ me[0], some] = act[:, k * width : (k + 1) * width]
        low_ref[some] = grad.astype(BF16)
        return total + jnp.sum(grad, axis=0, keepdims=True)

    bias_ref[...] = lax.fori_loop(0, rows // step, slab, jnp.zeros((1, w_ref.shape[1]), F32))


def middle(me, agg, cot, weight, bias):
    owners, rows, width = agg.shape
    full = owners * width
    inner = owners // OUTER
    block = inner * width
    return pl.pallas_call(
        middle_kernel,
        name="middle",
        out_shape=(
            jax.ShapeDtypeStruct((OUTER, inner, rows, width), BF16),
            jax.ShapeDtypeStruct((rows, full), BF16),
            jax.ShapeDtypeStruct((1, full), F32),
        ),
        grid_spec=pltpu.PrefetchScalarGridSpec(
            num_scalar_prefetch=1,
            grid=(OUTER,),
            in_specs=[
                pl.BlockSpec((owners, rows, width), lambda g, me: (0, 0, 0)),
                pl.BlockSpec((inner, rows, width), lambda g, me: (g, 0, 0)),
                pl.BlockSpec((full, block), lambda g, me: (0, g)),
                pl.BlockSpec((1, block), lambda g, me: (0, g)),
            ],
            out_specs=(
                pl.BlockSpec((1, inner, rows, width), lambda g, me: (g, 0, 0, 0)),
                pl.BlockSpec((rows, block), lambda g, me: (0, g)),
                pl.BlockSpec((1, block), lambda g, me: (0, g)),
            ),
            scratch_shapes=[pltpu.VMEM((rows, full), BF16), pltpu.VMEM((rows, block), F32)],
        ),
        compiler_params=params(28),
        cost_estimate=cost(2 * rows * full * full, 2 * full * full + 8 * rows * full),
    )(me, agg, cot, weight, bias[None])


def turned_dot(agg_ref, low_ref):
    left = jnp.concatenate([agg_ref[s].T for s in range(agg_ref.shape[0])], axis=0)
    return dot(left, low_ref[...], 1, 0)


def clamped(i, first, count):
    return jnp.clip(i - first, 0, count - 1)


def outer_kernel(blocks, which, agg_ref, low_ref, *refs):
    total = refs[-1]
    total[...] = turned_dot(agg_ref, low_ref).astype(BF16)
    for k, out_ref in enumerate(refs[:-1]):

        @pl.when(pl.program_id(0) // blocks == k)
        def _():
            out_ref[...] = total[...]


def outer(which, agg, low):
    owners, rows, width = agg.shape
    full = owners * width
    step = DEEP
    share = full // CHUNKS
    blocks = share // step

    def target(k):
        return lambda i, which: (clamped(i, k * blocks, blocks), 0)

    return pl.pallas_call(
        functools.partial(outer_kernel, blocks),
        name="outer",
        out_shape=[jax.ShapeDtypeStruct((share, full // 2), BF16)] * CHUNKS,
        grid_spec=pltpu.PrefetchScalarGridSpec(
            num_scalar_prefetch=1,
            grid=(CHUNKS * blocks,),
            in_specs=[
                pl.BlockSpec((step // width, rows, width), lambda i, which: (i, 0, 0)),
                pl.BlockSpec((rows, full // 2), lambda i, which: (0, which[0])),
            ],
            out_specs=[pl.BlockSpec((step, full // 2), target(k)) for k in range(CHUNKS)],
            scratch_shapes=[pltpu.VMEM((step, full // 2), BF16)],
        ),
        compiler_params=params(20),
        cost_estimate=cost(rows * full * full, 4 * rows * full + full * full),
    )(which[None].astype(jnp.int32), agg, low)


def outer_halve_kernel(blocks, which, agg_ref, low_ref, *refs):
    i = pl.program_id(0)
    *outs, total = refs[-2 * CHUNKS - 1 :]
    total[...] = turned_dot(agg_ref, low_ref)
    for n, out_ref in enumerate(outs):
        came_ref = refs[n // 2]

        @pl.when(i // blocks == n)
        def _():
            out_ref[...] = (total[...] + came_ref[...].astype(F32)).astype(out_ref.dtype)


def outer_halve(which, side, agg, low, came, after=()):
    owners, rows, width = agg.shape
    full = owners * width
    step = DEEP
    half = full // CHUNKS // 2
    blocks = half // step

    def row(i, which):
        k = i // (2 * blocks)
        part = i // blocks % 2
        near = jnp.where(k == 0, which[1], which[2])
        return k * 2 * blocks + jnp.where(part == 0, 1 - near, near) * blocks + i % blocks

    def arrived(k):
        def index(i, which):
            inside = clamped(i, k * 2 * blocks, 2 * blocks) + k * 2 * blocks
            return (row(inside, which) - k * 2 * blocks, 0)

        return index

    def target(n):
        return lambda i, which: (clamped(i, n * blocks, blocks), 0)

    outs = pl.pallas_call(
        functools.partial(outer_halve_kernel, blocks),
        name="outer_halve",
        out_shape=[
            jax.ShapeDtypeStruct((half, full // 2), dtype) for dtype in (BF16, F32) * CHUNKS
        ],
        grid_spec=pltpu.PrefetchScalarGridSpec(
            num_scalar_prefetch=1,
            grid=(2 * CHUNKS * blocks,),
            in_specs=[
                pl.BlockSpec(
                    (step // width, rows, width), lambda i, which: (row(i, which), 0, 0)
                ),
                pl.BlockSpec((rows, full // 2), lambda i, which: (0, which[0])),
            ]
            + [pl.BlockSpec((step, full // 2), arrived(k)) for k in range(CHUNKS)]
            + anywhere(after),
            out_specs=[pl.BlockSpec((step, full // 2), target(n)) for n in range(2 * CHUNKS)],
            scratch_shapes=[pltpu.VMEM((step, full // 2), F32)],
        ),
        compiler_params=params(28),
        cost_estimate=cost(rows * full * full, 4 * rows * full + 4 * full * full),
    )(jnp.stack([which, *side]).astype(jnp.int32), agg, low, *came, *after)
    return outs[0::2], outs[1::2]


def back_kernel(low_ref, w_ref, *refs):
    out_ref = refs[-1]
    parts, _, width = out_ref.shape
    value = dot(low_ref[...], w_ref[...], 1, 1).astype(BF16)
    for k in range(parts):
        out_ref[k] = value[:, k * width : (k + 1) * width]


def back(low, weight, owners, after=()):
    rows, full = low.shape
    width = full // owners
    step = DEEP // 2
    return pl.pallas_call(
        back_kernel,
        name="back",
        out_shape=jax.ShapeDtypeStruct((owners, rows, width), BF16),
        grid=(full // step,),
        in_specs=[
            pl.BlockSpec((rows, full), lambda i: (0, 0)),
            pl.BlockSpec((step, full), lambda i: (i, 0)),
        ]
        + anywhere(after),
        out_specs=pl.BlockSpec((step // width, rows, width), lambda i: (i, 0, 0)),
        compiler_params=params(20),
        cost_estimate=cost(2 * rows * full * full, 2 * full * full + 4 * rows * full),
    )(low, weight, *after)


def split_kernel(value_ref, *refs):
    count = value_ref.shape[1]
    for j, out_ref in enumerate(refs[-count:]):
        out_ref[...] = value_ref[:, j]


def row_step(rows):
    return rows // 2 if rows % 32 == 0 else rows


def split(value, after=()):
    first, second, rows, width = value.shape
    step = row_step(rows)
    return pl.pallas_call(
        split_kernel,
        name="split",
        out_shape=[jax.ShapeDtypeStruct((first, rows, width), BF16)] * second,
        grid=(rows // step,),
        in_specs=[pl.BlockSpec((first, second, step, width), lambda i: (0, 0, i, 0))]
        + anywhere(after),
        out_specs=[pl.BlockSpec((first, step, width), lambda i: (0, i, 0))] * second,
        compiler_params=params(16),
        cost_estimate=cost(0, 4 * value.size),
    )(value, *after)


def swap_with(value, mask):
    count = lax.axis_size("feat")
    return lax.ppermute(value, "feat", [(i, i ^ mask) for i in range(count)])


def scatter(values):
    return [values[0]] + [swap_with(values[k], k) for k in range(1, len(values))]


def outer_exchange(value):
    inner = lax.axis_size("feat") // OUTER
    groups = [[k * inner + low for k in range(OUTER)] for low in range(inner)]
    return lax.all_to_all(
        value, "feat", split_axis=0, concat_axis=0, axis_index_groups=groups, tiled=True
    )


def gather_rows(me, inner, blocks, out_ref):
    for high, low, block in blocks:
        rows = block.shape[0]
        owner = high * inner + (me ^ low)
        out_ref[pl.ds(pl.multiple_of(owner * rows, 16), rows), :] = block[...]


def swap_feat(value, bit):
    return swap_with(value, 1 << bit)


def swap_rep(value):
    return lax.ppermute(value, "rep", [(0, 1), (1, 0)])


def exchange(packed):
    owners = lax.axis_size("feat")
    blocks = packed.reshape(owners, -1, packed.shape[-1])
    return lax.all_to_all(blocks, "feat", split_axis=0, concat_axis=0, tiled=True)


def place_kernel(count, where, *refs):
    out_ref = refs[-1]
    for k in range(count):

        @pl.when(pl.program_id(0) == k)
        def _():
            out_ref[...] = refs[k][...].astype(F32)


def place(where, pieces, before=None, after=()):
    count = len(pieces)
    rows, columns = pieces[0].shape
    step = min(rows, 256)
    steps = rows // step
    full = 2 * columns
    begun = () if before is None else (before,)

    def source(k):
        return lambda i, j, where: (jnp.where(i == k, j, jnp.where(i < k, 0, steps - 1)), 0)

    return pl.pallas_call(
        functools.partial(place_kernel, count),
        name="place",
        out_shape=jax.ShapeDtypeStruct((full, full), F32),
        grid_spec=pltpu.PrefetchScalarGridSpec(
            num_scalar_prefetch=1,
            grid=(count, steps),
            in_specs=[pl.BlockSpec((step, columns), source(k)) for k in range(count)]
            + anywhere(begun)
            + anywhere(after),
            out_specs=pl.BlockSpec(
                (step, columns), lambda i, j, where: (where[i] * steps + j, where[count + i])
            ),
        ),
        input_output_aliases={1 + count: 0} if begun else {},
        compiler_params=params(16),
        cost_estimate=cost(0, 6 * count * rows * columns),
    )(jnp.stack(where).astype(jnp.int32), *pieces, *begun, *after)


def halve_kernel(chunks, side, *refs):
    outs = refs[-2 * chunks :]
    for k in range(chunks):
        for part in range(2):
            kept, came = refs[4 * k + 2 * part], refs[4 * k + 2 * part + 1]
            out = outs[2 * k + part]
            out[...] = (kept[...].astype(F32) + came[...].astype(F32)).astype(out.dtype)


def halve(side, kept, came, after=()):
    chunks = len(kept)
    half, columns = kept[0].shape[0] // 2, kept[0].shape[1]
    step = min(half, 128)
    steps = half // step

    def source(k, part):
        return lambda i, side: ((side[k] if part else 1 - side[k]) * steps + i, 0)

    in_specs = []
    operands = []
    out_shape = []
    for k in range(chunks):
        for part in range(2):
            for value in (kept[k], came[k]):
                in_specs.append(pl.BlockSpec((step, columns), source(k, part)))
                operands.append(value)
        for dtype in (BF16, F32):
            out_shape.append(jax.ShapeDtypeStruct((half, columns), dtype))
    outs = pl.pallas_call(
        functools.partial(halve_kernel, chunks),
        name="halve",
        out_shape=tuple(out_shape),
        grid_spec=pltpu.PrefetchScalarGridSpec(
            num_scalar_prefetch=1,
            grid=(steps,),
            in_specs=in_specs + anywhere(after),
            out_specs=[pl.BlockSpec((step, columns), lambda i, side: (i, 0)) for _ in out_shape],
        ),
        compiler_params=params(16),
        cost_estimate=cost(2 * chunks * half * columns, 18 * chunks * half * columns),
    )(jnp.stack(side).astype(jnp.int32), *operands, *after)
    return outs[0::2], outs[1::2]


def pick_kernel(side, *refs):
    first, second = (refs[2 * k][...] + refs[2 * k + 1][...].astype(F32) for k in range(2))
    away_ref, own_ref = refs[-2:]

    @pl.when(side[0] == 0)
    def _():
        own_ref[...] = first
        away_ref[...] = second.astype(BF16)

    @pl.when(side[0] == 1)
    def _():
        own_ref[...] = second
        away_ref[...] = first.astype(BF16)


def pick(side, kept, came, after=()):
    rows, columns = kept[0].shape
    step = min(rows, 128)
    block = pl.BlockSpec((step, columns), lambda i, side: (i, 0))
    away, own = pl.pallas_call(
        pick_kernel,
        name="pick",
        out_shape=(
            jax.ShapeDtypeStruct((rows, columns), BF16),
            jax.ShapeDtypeStruct((rows, columns), F32),
        ),
        grid_spec=pltpu.PrefetchScalarGridSpec(
            num_scalar_prefetch=1,
            grid=(rows // step,),
            in_specs=[block] * 4 + anywhere(after),
            out_specs=(block, block),
        ),
        compiler_params=params(16),
        cost_estimate=cost(2 * rows * columns, 18 * rows * columns),
    )(side[None].astype(jnp.int32), kept[0], came[0], kept[1], came[1], *after)
    return [away], [own]


def sort_kernel(side, own_ref, other_ref, *refs):
    first_ref, second_ref = refs[-2:]

    @pl.when(side[0] == 0)
    def _():
        first_ref[...] = own_ref[...]
        second_ref[...] = other_ref[...]

    @pl.when(side[0] == 1)
    def _():
        first_ref[...] = other_ref[...]
        second_ref[...] = own_ref[...]


def sort(side, own, other, after=()):
    whole = pl.BlockSpec(own.shape, lambda i, side: (0, 0))
    return pl.pallas_call(
        sort_kernel,
        name="sort",
        out_shape=[jax.ShapeDtypeStruct(own.shape, BF16)] * 2,
        grid_spec=pltpu.PrefetchScalarGridSpec(
            num_scalar_prefetch=1,
            grid=(1,),
            in_specs=[whole, whole] + anywhere(after),
            out_specs=[whole, whole],
        ),
        compiler_params=params(16),
        cost_estimate=cost(0, 8 * own.size),
    )(side[None].astype(jnp.int32), own, other, *after)


def add_kernel(first_ref, second_ref, *refs):
    refs[-1][...] = first_ref[...] + second_ref[...]


def add(first, second, after=()):
    return pl.pallas_call(
        add_kernel,
        name="add",
        out_shape=jax.ShapeDtypeStruct(first.shape, F32),
        in_specs=[pl.BlockSpec(memory_space=pltpu.VMEM)] * 2 + anywhere(after),
        compiler_params=params(16),
        cost_estimate=cost(first.size, 12 * first.size),
    )(first, second, *after)


def close_kernel(chunks, *refs):
    for k in range(chunks):
        total = refs[2 * k][...] + refs[2 * k + 1][...].astype(F32)
        refs[len(refs) - chunks + k][...] = total.astype(BF16)


def close(kept, came, after=()):
    chunks = len(kept)
    pairs = [value for pair in zip(kept, came) for value in pair]
    return pl.pallas_call(
        functools.partial(close_kernel, chunks),
        name="close",
        out_shape=[jax.ShapeDtypeStruct(value.shape, BF16) for value in kept],
        in_specs=[pl.BlockSpec(memory_space=pltpu.VMEM) for _ in pairs] + anywhere(after),
        compiler_params=params(16),
        cost_estimate=cost(kept[0].size * chunks, 8 * kept[0].size * chunks),
    )(*pairs, *after)


def join_kernel(chunks, side, *refs):
    outs = refs[-chunks:]
    for k in range(chunks):
        for part in range(2):

            @pl.when(pl.program_id(0) == part)
            def _():
                outs[k][...] = refs[2 * k + part][...]


def join(side, own, other, after=()):
    chunks = len(own)
    rows, columns = own[0].shape
    step = min(rows, 256)
    steps = rows // step
    pairs = [value for pair in zip(own, other) for value in pair]

    def source(part):
        return lambda i, j, side: (jnp.where(i == part, j, 0 if part else steps - 1), 0)

    def target(k):
        return lambda i, j, side: (jnp.where(i == 0, side[k], 1 - side[k]) * steps + j, 0)

    return pl.pallas_call(
        functools.partial(join_kernel, chunks),
        name="join",
        out_shape=[jax.ShapeDtypeStruct((2 * rows, columns), BF16) for _ in own],
        grid_spec=pltpu.PrefetchScalarGridSpec(
            num_scalar_prefetch=1,
            grid=(2, steps),
            in_specs=[pl.BlockSpec((step, columns), source(n % 2)) for n in range(2 * chunks)]
            + anywhere(after),
            out_specs=[pl.BlockSpec((step, columns), target(k)) for k in range(chunks)],
        ),
        compiler_params=params(16),
        cost_estimate=cost(0, 8 * chunks * rows * columns),
    )(jnp.stack(side).astype(jnp.int32), *pairs, *after)


def run(tiles, features, adjacency, counts, offsets, weight, bias, cotangent):
    owners = lax.axis_size("feat")
    me = lax.axis_index("feat")
    core = lax.axis_index("rep")
    bits = owners.bit_length() - 1
    inner = owners // OUTER
    side = [(me >> bit) & 1 for bit in range(bits)]
    crossed = [1, 0]
    low_bits = (me & (inner - 1)).astype(jnp.int32)
    place_of = low_bits[None]

    cot = pack(tiles, counts, offsets, cotangent)
    agg = exchange(aggregate(tiles, counts, offsets, features, adjacency, cot))
    cot = exchange(cot)
    act, low, grad_bias = middle(place_of, agg, cot, weight, bias)
    sent = outer(1 - core, agg, low)
    came = [swap_rep(value) for value in sent]
    act, _ = lax.optimization_barrier((act, sent[0]))
    act = outer_exchange(act)

    came_bias = swap_rep(grad_bias)
    away, kept = outer_halve(core, side[:2], agg, low, came)
    came = [swap_feat(away[k], k) for k in range(2)]
    back_rows = back(low, weight, owners, away)
    grad_bias = add(grad_bias, came_bias, (back_rows,))
    came_bias = swap_feat(grad_bias, 0)
    away, kept = halve([side[1], side[0]], kept, came, (grad_bias,))
    came = [swap_feat(away[k], crossed[k]) for k in range(2)]
    grad_bias = add(grad_bias, came_bias, away)
    came_bias = swap_feat(grad_bias, 1)
    away, kept = pick(side[2], kept, came, (grad_bias,))
    came = [swap_feat(away[0], 2)]
    act = split(act, away)
    grad_bias = add(grad_bias, came_bias, (act[0],))
    act = scatter(act)
    for bit in range(3, bits):
        came_bias = swap_feat(grad_bias, bit - 1)
        away, kept = halve(side[bit : bit + 1], kept, came, (grad_bias,))
        came = [swap_feat(away[0], bit)]
        grad_bias = add(grad_bias, came_bias, away)
    came_bias = swap_feat(grad_bias, bits - 1)
    grad_bias = add(grad_bias, came_bias, away)
    owned = close(kept, came, (grad_bias,))
    for bit in reversed(range(3, bits)):
        owned = join(side[bit : bit + 1], owned, [swap_feat(owned[0], bit)])
    other = swap_feat(owned[0], 2)
    activations = unpack(features.shape, counts, offsets, place_of, act, owned)
    owned = sort(side[2], owned[0], other, (activations,))
    other = [swap_feat(owned[k], crossed[k]) for k in range(2)]
    back_rows, owned = lax.optimization_barrier((back_rows, owned))
    back_rows = exchange(back_rows).reshape(tiles * TILE, -1)
    owned = join([side[1], side[0]], owned, other)
    across = [swap_rep(value) for value in owned]
    far = [swap_feat(owned[k], k) for k in range(2)]
    near_rows = [2 * k + side[k] for k in range(2)]
    far_rows = [2 * k + 1 - side[k] for k in range(2)]
    columns = [core] * 2 + [1 - core] * 2
    grad_weight = place(2 * near_rows + columns, [*owned, *across])
    grad_features = spread(counts, offsets, back_rows, adjacency, (grad_weight,))
    far, grad_features = lax.optimization_barrier((far, grad_features))
    far_across = [swap_rep(value) for value in far]
    grad_weight = place(far_rows + columns[:2], far, grad_weight)
    grad_weight = place(far_rows + columns[2:], far_across, grad_weight)
    return activations, grad_features, grad_weight, grad_bias[0]


def local(features, adjacency, counts, weight, bias, cotangent):
    features = features.transpose(1, 0, 2)
    cotangent = cotangent.transpose(1, 0, 2)
    clusters, _, nodes = features.shape
    used = (counts + TILE - 1) // TILE
    before = jnp.arange(clusters)[None] < jnp.arange(clusters + 1)[:, None]
    offsets = jnp.sum(jnp.where(before, used[None], 0), axis=1).astype(jnp.int32)
    need = offsets[-1:]
    need = jnp.maximum(need, swap_rep(need))[0]
    most = clusters * nodes // TILE
    unit = max(2, 16 * lax.axis_size("feat") // TILE)
    buckets = [b for b in BUCKETS if b < most and b % unit == 0] + [most]
    ordered = sorted(buckets)
    branch = jnp.int32(buckets.index(ordered[0]))
    for low, high in zip(ordered, ordered[1:]):
        branch = jnp.where(need > low, buckets.index(high), branch)
    branches = [functools.partial(run, b) for b in buckets]
    args = (features, adjacency, counts, offsets, weight, bias, cotangent)
    activations, grad_features, grad_weight, grad_bias = lax.switch(branch, branches, *args)
    return (
        activations.transpose(1, 0, 2),
        grad_features.transpose(1, 0, 2),
        grad_weight,
        grad_bias,
    )


def solution(mesh):
    placed = (
        P("feat", "rep", None),
        P("rep", None, None),
        P("rep"),
        P(),
        P(),
        P("feat", "rep", None),
    )
    return jax.shard_map(
        local,
        mesh=mesh,
        in_specs=placed,
        out_specs=(P("feat", "rep", None), P("feat", "rep", None), P(), P()),
        check_vma=False,
    )
```
